512 devices in a mesh: layer: 4 (over y_lo), latent: 128 (over x, z, y_hi, core).
Axes of the slice: x: 4, y: 8 (y_hi: 2, y_lo: 4; y = y_hi * 4 + y_lo), z: 8, core: 2. Of those that a mesh axis runs over, the one named last changes fastest.
Arguments:
- inputs: bfloat16 [4, 192, 5120], P('layer', None, 'latent'), may hold values from -6 to 6
- targets: bfloat16 [4, 192, 5120], P('layer', None, 'latent'), may hold values from -6 to 6
- encoder: bfloat16 [4, 8192, 5120], P('layer', 'latent'), may hold values from -0.078125 to 0.078125
- threshold: float32 [4, 8192], P('layer', 'latent'), may hold values from 0.1 to 1
- decoders: bfloat16 [4, 4, 8192, 5120], P('layer', None, 'latent'), may hold values from -0.25 to 0.25
- out_bias: bfloat16 [4, 5120], P('layer', 'latent'), may hold values from -3 to 3
- positions: int32 [192], replicated, may hold values from 0 to 95, as said below
Outputs:
- grad_encoder: float32 [4, 8192, 5120], P('layer', 'latent')
- grad_threshold: float32 [4, 8192], P('layer', 'latent')
The draws below stay inside these ranges and needn't reach their ends.
Inputs may be any that keep to these rules, and one draw needn't show every extreme that they name: `positions`: each token's position within its packed document; the first document covers exactly the first 96 tokens, and later documents start in the second half.
All inputs are finite; a program needn't handle non-finite values.
Results may differ from the reference program's by a relative error of at most 0.0045.
Values may be sent and summed in bfloat16 or wider, within the bound.
No kernel may reach another device: no remote copies, remote signals or barrier semaphores. Data moves between devices by JAX's collectives and lax.ppermute only.
A program may use at most 64 MiB of HBM per device.

```python
import math
import jax
import jax.numpy as jnp
from jax import lax

D = 5120
F = 8192
TOK = 192
LAYERS = 4


def draw_positions(key, part):
    key = jax.random.fold_in(key, 11)
    flags = jax.random.randint(key, (TOK,), 0, 8)
    index = jnp.arange(TOK, dtype=jnp.int32)
    half = TOK // 2
    opens = (index == 0) | (index == half) | (flags == 0) & (index > half)
    starts = jnp.where(opens, index, 0).astype(jnp.int32)
    return (index - lax.cummax(starts)).astype(jnp.int32)


def raised(values, rng, source, target, parts, factor):
    owner, partner = [(jnp.arange(values.shape[position]) // (values.shape[position] // parts)).reshape([-1 if axis == position else 1 for axis in range(values.ndim)]) for position in (source, target)]
    chosen = jax.random.permutation(rng, parts)[partner]
    strong = (owner == chosen) | (owner == (partner + parts // 2) % parts)
    return jnp.where(strong, factor * values, values)


def level_of(rng, dims, shards, smallest, high):
    def one(dim, parts):
        draws = jax.random.uniform(jax.random.fold_in(jax.random.fold_in(rng, 6), dim), (parts,), jnp.float32, smallest / len(shards), high / len(shards))
        return jnp.repeat(jnp.exp(draws), dims[dim] // parts).reshape((-1,) + (1,) * (len(dims) - dim - 1))

    gain = one(*shards[0])
    for cut in shards[1:]:
        gain = gain * one(*cut)
    return gain


def gaussian(key, extent, spread, limit, shards=(), kind=jnp.bfloat16):
    entries = jax.random.normal(key, extent, jnp.float32) * spread
    if len(shards) > 0:
        entries = level_of(key, extent, shards, -0.22, 0.18) * entries
    return jnp.clip(entries, min=-limit, max=limit).astype(kind)


def noise_with(own_key, shape, width, bound, cuts, heavy, kind=jnp.bfloat16):
    array = width * jax.random.normal(own_key, shape, jnp.float32)
    if cuts:
        array = array * level_of(own_key, shape, cuts, -0.22, 0.18)
    return jnp.clip(raised(array, jax.random.fold_in(own_key, 3), *heavy), -bound, bound).astype(kind)


def setup_inputs(seed: int = 0) -> dict:
    keys = jax.random.split(jax.random.key(seed), 8)
    return {
        "inputs": gaussian(keys[0], (LAYERS, TOK, D), 1.0, 6.0, ((0, 4), (2, 128))),
        "targets": gaussian(keys[1], (LAYERS, TOK, D), 1.0, 6.0, ((0, 4), (2, 128))),
        "encoder": gaussian(keys[2], (LAYERS, F, D), D ** -0.5, 0.078125, ((0, 4), (1, 128))),
        "threshold": jnp.clip(jnp.exp(math.log(1.0) - 2.3025851 * jax.random.uniform(keys[3], (LAYERS, F), jnp.float32) ** level_of(keys[3], (LAYERS, F), ((0, 4), (1, 128)), -0.2, 0.2)), 0.1, 1.0),
        "decoders": noise_with(keys[4], (LAYERS, LAYERS, F, D), F ** -0.5, 0.25, ((0, 4), (2, 128)), (2, 3, 128, 5.5)),
        "out_bias": gaussian(keys[5], (LAYERS, D), 0.5, 3.0, ((0, 4), (1, 128))),
        "positions": draw_positions(jax.random.fold_in(keys[7], 71), 0),
    }


def smooth_gate(shifted):
    sig = jax.nn.sigmoid(4.0 * shifted)
    return shifted * sig, sig + 4.0 * shifted * sig * (1.0 - sig)


def reference(inputs, targets, encoder, threshold, decoders, out_bias, positions):
    token_mask = (positions > 0).astype(jnp.float32)[:, None]
    code_list = []
    slope_list = []
    for source in range(LAYERS):
        preact = lax.dot_general(inputs[source], encoder[source], (((1,), (1,)), ((), ())), preferred_element_type=jnp.float32)
        activity, gate_slope = smooth_gate(preact - threshold[source][None, :])
        code_list.append(activity.astype(jnp.bfloat16))
        slope_list.append(gate_slope)
    error_list = []
    for target in range(LAYERS):
        recon_sum = jnp.zeros((TOK, D), jnp.float32)
        for source in range(target + 1):
            recon_sum = recon_sum + jnp.dot(code_list[source], decoders[target, source], preferred_element_type=jnp.float32)
        error_full = token_mask * (recon_sum + out_bias[target].astype(jnp.float32)[None, :] - targets[target].astype(jnp.float32)) / LAYERS
        error_list.append(error_full.astype(jnp.bfloat16))
    grad_list = []
    thresh_list = []
    for source in range(LAYERS):
        code_grad = jnp.zeros((TOK, F), jnp.float32)
        for target in range(source, LAYERS):
            code_grad = code_grad + lax.dot_general(error_list[target], decoders[target, source], (((1,), (1,)), ((), ())), preferred_element_type=jnp.float32)
        z_grad = code_grad * slope_list[source]
        thresh_list.append(-jnp.sum(z_grad, axis=0))
        grad_list.append(lax.dot_general(z_grad.astype(jnp.bfloat16), inputs[source], (((0,), (0,)), ((), ())), preferred_element_type=jnp.float32))
    return jnp.stack(grad_list), jnp.stack(thresh_list)
```

```python
import jax
import jax.numpy as jnp
from jax import lax
from jax.sharding import Mesh, PartitionSpec as P

F32 = jnp.float32
BF16 = jnp.bfloat16


def smooth_gate(shifted):
    sig = jax.nn.sigmoid(4.0 * shifted)
    return (shifted * sig, sig + 4.0 * shifted * sig * (1.0 - sig))


def size_of(axes):
    count = 1
    for name in axes:
        count *= lax.axis_size(name)
    return count


def spread(block, axes):
    count = size_of(axes)
    copies = jnp.broadcast_to(block[None], (count,) + block.shape)
    return lax.all_to_all(copies, axes, 0, 0, tiled=True)


def swap(block):
    return lax.ppermute(block, "core", [(0, 1), (1, 0)])


def body(inputs, targets, encoder, threshold, decoders, out_bias, positions):
    layers = lax.axis_size("layer")
    section = lax.axis_index("layer")
    first = lax.axis_index("core") == 0
    inputs_t = inputs[0].T
    targets_t = targets[0].T
    width, tokens = inputs_t.shape
    half = tokens // 2
    latents = threshold.shape[1]

    def mine(array):
        return jnp.where(first, array[:, :half], array[:, half:])

    def other(array):
        return jnp.where(first, array[:, half:], array[:, :half])

    def row(vector):
        return jnp.pad(vector.astype(F32), (0, half - vector.shape[0]))[None]

    rows = jnp.concatenate([row(out_bias[0]), row(threshold[0])], axis=0)
    packed = jnp.concatenate([other(inputs_t).astype(F32), other(targets_t).astype(F32), rows], axis=0)
    received = swap(packed)
    other_encoder = swap(encoder[0])
    other_decoders = swap(decoders[0])

    def pair(own, sent):
        return jnp.where(first, jnp.concatenate([own, sent], axis=0), jnp.concatenate([sent, own], axis=0))

    own_inputs = pair(mine(inputs_t), received[:width].astype(BF16))
    own_targets = pair(mine(targets_t).astype(F32), received[width : 2 * width])
    own_bias = pair(out_bias[0].astype(F32), received[2 * width, :width])
    other_threshold = received[2 * width + 1, :latents]
    own_mask = mine((positions > 0).astype(F32)[None, :])

    block = spread(own_inputs, ("z", "yh")).reshape(-1, half)
    whole_inputs = spread(block, ("x",)).reshape(-1, half)
    other_inputs = swap(whole_inputs)

    def encode(part, bias):
        preact = lax.dot_general(part, whole_inputs, (((1,), (0,)), ((), ())), preferred_element_type=F32)
        return smooth_gate(preact - bias[:, None])

    activity_a, slope_a = encode(encoder[0], threshold[0])
    activity_b, slope_b = encode(other_encoder, other_threshold)
    code_block = jnp.concatenate([activity_a.astype(BF16), activity_b.astype(BF16)], axis=0)
    codes = spread(code_block, ("layer",))
    earlier = (jnp.arange(layers, dtype=jnp.int32) <= section)[:, None, None]
    codes = jnp.where(earlier, codes, jnp.zeros_like(codes))

    def decode(part, code):
        return lax.dot_general(part, code, (((0, 1), (0, 1)), ((), ())), preferred_element_type=F32)

    recon = decode(decoders[0], codes[:, :latents]) + decode(other_decoders, codes[:, latents:])
    recon = recon.astype(BF16)
    count_x = lax.axis_size("x")
    recon = lax.all_to_all(recon.reshape(count_x, -1, half), ("x",), 0, 0, tiled=True)
    recon = jnp.sum(recon.astype(F32), axis=0)
    recon = lax.all_to_all(recon.reshape(size_of(("z", "yh")), -1, half), ("z", "yh"), 0, 0, tiled=True)
    recon = jnp.sum(recon, axis=0)
    error = (own_mask * (recon + own_bias[:, None] - own_targets) / layers).astype(BF16)
    block = spread(error, ("z", "yh")).reshape(-1, half)
    error_full = spread(block, ("x",)).reshape(-1, half)

    def back(part):
        return lax.dot_general(part, error_full, (((2,), (0,)), ((), ())), preferred_element_type=F32)

    back_terms = jnp.concatenate([back(decoders[0]), back(other_decoders)], axis=1)
    back_terms = jnp.where(earlier, back_terms, jnp.zeros_like(back_terms))
    code_grad = jnp.sum(lax.all_to_all(back_terms, ("layer",), 0, 0, tiled=True), axis=0)
    z_a = code_grad[:latents] * slope_a
    z_b = code_grad[latents:] * slope_b
    z_c = swap(z_b)
    grad_threshold = -jnp.sum(z_a + z_c, axis=1)

    def outer(grad, source):
        return lax.dot_general(grad.astype(BF16), source, (((1,), (1,)), ((), ())), preferred_element_type=F32)

    grad_encoder = outer(z_a, whole_inputs) + outer(z_c, other_inputs)
    return (grad_encoder[None], grad_threshold[None])


LATENT = ("x", "z", "yh", "core")


def split_mesh(mesh, parts):
    devices = mesh.devices.reshape((mesh.devices.shape[0],) + parts)
    return Mesh(devices, ("layer",) + LATENT)


def solution(mesh, parts=(4, 8, 2, 2)):
    in_specs = (
        P("layer", None, LATENT),
        P("layer", None, LATENT),
        P("layer", LATENT, None),
        P("layer", LATENT),
        P("layer", None, LATENT, None),
        P("layer", LATENT),
        P(),
    )
    out_specs = (P("layer", LATENT, None), P("layer", LATENT))
    fine = split_mesh(mesh, parts)
    return jax.shard_map(body, mesh=fine, in_specs=in_specs, out_specs=out_specs, check_vma=False)
```

```python
import jax
import jax.numpy as jnp
from jax import lax
from jax.sharding import Mesh, PartitionSpec as P

F32 = jnp.float32
BF16 = jnp.bfloat16
NEAR = ("x", "zl")
FAR = ("zh", "yh")


def smooth_gate(shifted):
    sig = jax.nn.sigmoid(4.0 * shifted)
    return (shifted * sig, sig + 4.0 * shifted * sig * (1.0 - sig))


def size_of(axes):
    count = 1
    for name in axes:
        count *= lax.axis_size(name)
    return count


def exchange(blocks, axes):
    return lax.all_to_all(blocks, axes, 0, 0, tiled=True)


def spread(block, axes):
    return exchange(jnp.broadcast_to(block[None], (size_of(axes),) + block.shape), axes)


def swap(block):
    return lax.ppermute(block, "core", [(0, 1), (1, 0)])


def to_owner(block):
    high, low = lax.axis_size("zh"), lax.axis_size("zl")
    pairs = [(a * high + b, b * low + a) for a in range(low) for b in range(high)]
    return lax.ppermute(block, ("zh", "zl"), pairs)


def body(inputs, targets, encoder, threshold, decoders, out_bias, positions):
    layers = lax.axis_size("layer")
    section = lax.axis_index("layer")
    first = lax.axis_index("core") == 0
    width, tokens = inputs.shape[2], inputs.shape[1]
    half = tokens // 2
    latents = threshold.shape[1]
    xs, zh, zl, yh = (lax.axis_size(name) for name in ("x", "zh", "zl", "yh"))

    def halves(array):
        return jnp.stack([array[:, :half], array[:, half:]])

    def mine(pair):
        return jnp.where(first, pair[0], pair[1])

    def other(pair):
        return jnp.where(first, pair[1], pair[0])

    input_halves = halves(inputs[0].T)
    sends = jnp.broadcast_to(input_halves[None], (zh * yh,) + input_halves.shape)
    block = exchange(sends.reshape((-1, width, half)), FAR + ("core",)).reshape(-1, half)

    def row(vector):
        return jnp.pad(vector.astype(F32), (0, half - vector.shape[0]))[None]

    target_halves = halves(targets[0].T).astype(F32)
    rows = jnp.concatenate([row(out_bias[0]), row(threshold[0])], axis=0)
    received = swap(jnp.concatenate([other(target_halves), rows], axis=0))
    other_encoder = swap(encoder[0])
    other_decoders = swap(decoders[0])
    other_threshold = received[width + 1, :latents]

    def both(own, sent):
        return jnp.where(first, jnp.concatenate([own, sent], axis=0), jnp.concatenate([sent, own], axis=0))

    own_targets = both(mine(target_halves), received[:width])
    own_bias = both(out_bias[0].astype(F32), received[width, :width])
    offset = to_owner(own_targets - own_bias[:, None])
    own_mask = mine(halves((positions > 0).astype(F32)[None, :]))

    whole_inputs = spread(block, NEAR).reshape(xs, zl, zh, yh * 2 * width, half)
    whole_inputs = whole_inputs.transpose(0, 2, 1, 3, 4).reshape(-1, half)
    other_inputs = swap(whole_inputs)

    def encode(part, bias):
        preact = lax.dot_general(part, whole_inputs, (((1,), (0,)), ((), ())), preferred_element_type=F32)
        return smooth_gate(preact - bias[:, None])

    activity_a, slope_a = encode(encoder[0], threshold[0])
    activity_b, slope_b = encode(other_encoder, other_threshold)
    slope_c = swap(slope_b)
    code_block = jnp.concatenate([activity_a.astype(BF16), activity_b.astype(BF16)], axis=0)
    codes = spread(code_block, ("layer",))
    earlier = (jnp.arange(layers, dtype=jnp.int32) <= section)[:, None, None]
    codes = jnp.where(earlier, codes, jnp.zeros_like(codes))

    def decode(part, code):
        return lax.dot_general(part, code, (((0, 1), (0, 1)), ((), ())), preferred_element_type=F32)

    recon = decode(decoders[0], codes[:, :latents]) + decode(other_decoders, codes[:, latents:])
    recon = exchange(recon.astype(BF16).reshape(xs * zl, -1, half), NEAR)
    recon = jnp.sum(recon.astype(F32), axis=0)
    recon = exchange(recon.reshape(zh * yh, -1, half), FAR)
    recon = jnp.sum(recon, axis=0)
    error = (own_mask * (recon - offset) / layers).astype(BF16)
    block = spread(error, FAR).reshape(-1, half)
    error_full = spread(block, NEAR).reshape(-1, half)

    def back(part):
        return lax.dot_general(part, error_full, (((2,), (0,)), ((), ())), preferred_element_type=F32)

    back_a, back_b = back(decoders[0]), back(other_decoders)
    back_terms = jnp.stack([jnp.where(first, back_a, back_b), jnp.where(first, back_b, back_a)], axis=1)
    back_terms = jnp.where(earlier[:, None], back_terms, jnp.zeros_like(back_terms))
    code_grad = exchange(back_terms.reshape((-1, latents, half)), ("layer", "core"))
    code_grad = jnp.sum(code_grad.reshape(layers, 2, latents, half), axis=0)
    z_a = mine(code_grad) * slope_a
    z_c = other(code_grad) * slope_c
    grad_threshold = -jnp.sum(z_a + z_c, axis=1)

    def outer(grad, source):
        return lax.dot_general(grad.astype(BF16), source, (((1,), (1,)), ((), ())), preferred_element_type=F32)

    grad_encoder = outer(z_a, whole_inputs) + outer(z_c, other_inputs)
    return (grad_encoder[None], grad_threshold[None])


LATENT = ("x", "zh", "zl", "yh", "core")


def solution(mesh, parts=(4, 4, 2, 2, 2)):
    in_specs = (
        P("layer", None, LATENT),
        P("layer", None, LATENT),
        P("layer", LATENT, None),
        P("layer", LATENT),
        P("layer", None, LATENT, None),
        P("layer", LATENT),
        P(),
    )
    out_specs = (P("layer", LATENT, None), P("layer", LATENT))
    devices = mesh.devices.reshape((mesh.devices.shape[0],) + parts)
    fine = Mesh(devices, ("layer",) + LATENT)
    return jax.shard_map(body, mesh=fine, in_specs=in_specs, out_specs=out_specs, check_vma=False)
```

```python
import functools

import jax
import jax.numpy as jnp
from jax import lax
from jax.experimental import pallas as pl
from jax.experimental.pallas import tpu as pltpu
from jax.sharding import Mesh, PartitionSpec as P

F32 = jnp.float32
BF16 = jnp.bfloat16
NEAR = ("x", "zl")
FAR = ("zh", "yh")
ANY = pl.BlockSpec(memory_space=pl.ANY)
VMEM = pl.BlockSpec(memory_space=pltpu.VMEM)
MIB = 1 << 20


def dot(left, right, dims):
    return lax.dot_general(left, right, (dims, ((), ())), preferred_element_type=F32)


def size_of(axes):
    count = 1
    for name in axes:
        count *= lax.axis_size(name)
    return count


def exchange(blocks, axes):
    return lax.all_to_all(blocks, axes, 0, 0, tiled=True)


def swap(block):
    return lax.ppermute(block, "core", [(0, 1), (1, 0)])


def to_owner(block):
    high, low = lax.axis_size("zh"), lax.axis_size("zl")
    pairs = [(a * high + b, b * low + a) for a in range(low) for b in range(high)]
    return lax.ppermute(block, ("zh", "zl"), pairs)


def call(kernel, outs, operands, later=(), mib=16, flops=0):
    def run(*refs):
        kernel(*refs[: len(operands)], *refs[len(operands) + len(later) :])

    size = sum(o.size * o.dtype.itemsize for o in list(outs) + list(operands))
    return pl.pallas_call(
        run,
        out_shape=outs,
        in_specs=[VMEM] * len(operands) + [ANY] * len(later),
        out_specs=[VMEM] * len(outs),
        compiler_params=pltpu.CompilerParams(vmem_limit_bytes=mib * MIB),
        cost_estimate=pl.CostEstimate(flops=flops, bytes_accessed=size, transcendentals=0),
    )(*operands, *later)


def struct(shape, dtype):
    return jax.ShapeDtypeStruct(shape, dtype)


def flip_kernel(block_ref, out_ref):
    block = block_ref[...].astype(F32).T.astype(BF16)
    for k in range(out_ref.shape[0]):
        out_ref[k] = block


def encode_kernel(sizes, blocks_ref, own_ref, sent_ref, own_bias, sent_bias, whole_ref, code_ref, own_slope, sent_slope):
    xs, zh, zl, rest = sizes
    for x in range(xs):
        parts = [
            blocks_ref[x * zl + low, :, high * rest : (high + 1) * rest] for high in range(zh) for low in range(zl)
        ]
        width = len(parts) * rest
        whole_ref[:, x * width : (x + 1) * width] = jnp.concatenate(parts, axis=1)
    whole = whole_ref[...]
    codes = []
    for part, bias, slope in ((own_ref, own_bias, own_slope), (sent_ref, sent_bias, sent_slope)):
        shifted = dot(part[...], whole, ((1,), (1,))) - bias[...]
        sig = jax.nn.sigmoid(4.0 * shifted)
        slope[...] = sig + 4.0 * shifted * sig * (1.0 - sig)
        codes.append(shifted * sig)
    code = jnp.concatenate(codes, axis=0).T.astype(BF16)
    for layer in range(code_ref.shape[0]):
        code_ref[layer] = code


def decode_kernel(codes_ref, own_ref, sent_ref, out_ref):
    section = lax.axis_index("layer")
    layers, _, latents = codes_ref.shape
    latents //= 2
    codes = []
    for layer in range(layers):
        code = codes_ref[layer]
        codes.append(jnp.where(layer <= section, code, jnp.zeros_like(code)))
    own = jnp.concatenate([code[:, :latents] for code in codes], axis=1)
    sent = jnp.concatenate([code[:, latents:] for code in codes], axis=1)
    count, _, width = out_ref.shape
    for k in range(count):
        part = slice(k * width, (k + 1) * width)
        total = dot(own, own_ref[:, part], ((1,), (0,))) + dot(sent, sent_ref[:, part], ((1,), (0,)))
        out_ref[k] = total.astype(BF16)


def reduce_kernel(rows, parts_ref, offset_ref, out_ref):
    total = -offset_ref[...]
    for k in range(parts_ref.shape[0]):
        total += parts_ref[k].astype(F32)
    for k in range(out_ref.shape[0]):
        out_ref[k, :rows] = total[k * rows : (k + 1) * rows]
        if rows < out_ref.shape[1]:
            out_ref[k, rows:] = jnp.zeros((out_ref.shape[1] - rows, out_ref.shape[2]), F32)


def error_kernel(scale, parts_ref, mask_ref, out_ref):
    total = parts_ref[0]
    for k in range(1, parts_ref.shape[0]):
        total += parts_ref[k]
    error = (mask_ref[...] * total * scale).astype(BF16)
    for k in range(out_ref.shape[0]):
        out_ref[k] = error


def repeat_kernel(rows, parts_ref, out_ref):
    parts = [parts_ref[k].astype(F32)[:rows] for k in range(parts_ref.shape[0])]
    block = jnp.concatenate(parts, axis=0).astype(BF16)
    for k in range(out_ref.shape[0]):
        out_ref[k] = block


def back_kernel(error_ref, own_ref, sent_ref, out_ref):
    section = lax.axis_index("layer")
    first = lax.axis_index("core") == 0
    error = jnp.concatenate([error_ref[k] for k in range(error_ref.shape[0])], axis=1)
    own = dot(own_ref[...], error, ((1,), (1,)))
    sent = dot(sent_ref[...], error, ((1,), (1,)))
    latents = out_ref.shape[1]
    for layer in range(out_ref.shape[0] // 2):
        rows = slice(layer * latents, (layer + 1) * latents)
        kept = (layer <= section).astype(F32)
        out_ref[2 * layer] = jnp.where(first, own[rows], sent[rows]) * kept
        out_ref[2 * layer + 1] = jnp.where(first, sent[rows], own[rows]) * kept


def final_kernel(terms_ref, own_slope, sent_slope, own_ref, sent_ref, grad_ref, threshold_ref):
    first = lax.axis_index("core") == 0
    low, high = terms_ref[0], terms_ref[1]
    for k in range(2, terms_ref.shape[0], 2):
        low += terms_ref[k]
        high += terms_ref[k + 1]
    own = jnp.where(first, low, high) * own_slope[...]
    sent = jnp.where(first, high, low) * sent_slope[...]
    total = -jnp.sum(own + sent, axis=1, keepdims=True)
    threshold_ref[...] = jnp.broadcast_to(total, (total.shape[0], 128)).T[:1]
    grad = dot(own.astype(BF16), own_ref[...], ((1,), (0,)))
    grad_ref[...] = grad + dot(sent.astype(BF16), sent_ref[...], ((1,), (0,)))


def body(inputs, targets, encoder, threshold, decoders, out_bias, positions):
    layers = lax.axis_size("layer")
    first = lax.axis_index("core") == 0
    width, tokens = inputs.shape[2], inputs.shape[1]
    half = tokens // 2
    latents, model = encoder.shape[1], encoder.shape[2]
    xs, zh, zl, yh = (lax.axis_size(name) for name in ("x", "zh", "zl", "yh"))
    near, far = xs * zl, zh * yh
    wide, rows = model // near, half // far
    tall = -(-rows // 16) * 16
    place = lax.axis_index(FAR)

    def halves(array):
        return jnp.stack([array[:, :half], array[:, half:]])

    def mine(pair):
        return jnp.where(first, pair[0], pair[1])

    def other(pair):
        return jnp.where(first, pair[1], pair[0])

    input_halves = halves(inputs[0].T)
    sends = jnp.broadcast_to(input_halves[None], (far,) + input_halves.shape)
    block = exchange(sends.reshape((-1, width, half)), FAR + ("core",)).reshape(-1, half)

    def row(vector):
        return jnp.pad(vector.astype(F32), (0, half - vector.shape[0]))[None]

    target_halves = halves(targets[0].T).astype(F32)
    sides = jnp.concatenate([row(out_bias[0]), row(threshold[0])], axis=0)
    received = swap(jnp.concatenate([other(target_halves), sides], axis=0))
    other_encoder = swap(encoder[0])
    own_decoders = decoders[0].reshape(layers * latents, model)
    other_decoders = swap(own_decoders)
    other_threshold = received[width + 1, :latents]

    def both(own, sent):
        return jnp.where(first, jnp.concatenate([own, sent], axis=0), jnp.concatenate([sent, own], axis=0))

    own_targets = both(mine(target_halves), received[:width])
    own_bias = both(out_bias[0].astype(F32), received[width, :width])
    offset = to_owner(own_targets - own_bias[:, None])

    (sends,) = call(
        flip_kernel, [struct((near, half, wide), BF16)], [block], later=[received, other_encoder, other_decoders]
    )
    blocks = exchange(sends, NEAR)
    tile = jnp.tile(offset.T, (1, far))
    lane = lax.broadcasted_iota(jnp.int32, tile.shape, 1) // (2 * width)
    offset = jnp.where(lane == place, tile, jnp.zeros_like(tile))
    token_mask = (positions > 0).astype(F32)
    start = lax.axis_index("core") * half + place * rows
    own_mask = jnp.pad(lax.dynamic_slice(token_mask, (start,), (rows,)), (0, tall - rows))[:, None]

    whole, codes, own_slope, sent_slope = call(
        functools.partial(encode_kernel, (xs, zh, zl, wide // zh)),
        [
            struct((half, model), BF16),
            struct((layers, half, 2 * latents), BF16),
            struct((latents, half), F32),
            struct((latents, half), F32),
        ],
        [blocks, encoder[0], other_encoder, threshold[0][:, None], other_threshold[:, None]],
        flops=4 * half * latents * model,
    )
    codes = exchange(codes, ("layer",))
    other_whole = swap(whole)
    other_slope = swap(sent_slope)

    (parts,) = call(
        decode_kernel,
        [struct((near, half, wide), BF16)],
        [codes, own_decoders, other_decoders],
        flops=4 * layers * half * latents * model,
    )
    parts = exchange(parts, NEAR)
    (parts,) = call(
        functools.partial(reduce_kernel, rows),
        [struct((far, tall, wide), F32)],
        [parts, offset],
        later=[other_whole, other_slope],
    )
    parts = exchange(parts, FAR)
    (parts,) = call(
        functools.partial(error_kernel, 1.0 / layers), [struct((far, tall, wide), BF16)], [parts, own_mask]
    )
    parts = exchange(parts, FAR)
    (parts,) = call(functools.partial(repeat_kernel, rows), [struct((near, half, wide), BF16)], [parts])
    error = exchange(parts, NEAR)
    (terms,) = call(
        back_kernel,
        [struct((2 * layers, latents, half), F32)],
        [error, own_decoders, other_decoders],
        flops=4 * layers * half * latents * model,
    )
    terms = exchange(terms, ("layer", "core"))
    grad_encoder, grad_threshold = call(
        final_kernel,
        [struct((latents, model), F32), struct((1, latents), F32)],
        [terms, own_slope, other_slope, whole, other_whole],
        flops=4 * half * latents * model,
    )
    return (grad_encoder[None], grad_threshold)


LATENT = ("x", "zh", "zl", "yh", "core")


def solution(mesh, parts=(4, 4, 2, 2, 2)):
    in_specs = (
        P("layer", None, LATENT),
        P("layer", None, LATENT),
        P("layer", LATENT, None),
        P("layer", LATENT),
        P("layer", None, LATENT, None),
        P("layer", LATENT),
        P(),
    )
    out_specs = (P("layer", LATENT, None), P("layer", LATENT))
    devices = mesh.devices.reshape((mesh.devices.shape[0],) + parts)
    fine = Mesh(devices, ("layer",) + LATENT)
    return jax.shard_map(body, mesh=fine, in_specs=in_specs, out_specs=out_specs, check_vma=False)
```

```python
import functools

import jax
import jax.numpy as jnp
from jax import lax
from jax.experimental import pallas as pl
from jax.experimental.pallas import tpu as pltpu
from jax.sharding import Mesh, PartitionSpec as P

F32 = jnp.float32
BF16 = jnp.bfloat16
NEAR = ("x", "zl")
FAR = ("zh", "yh")
ANY = pl.BlockSpec(memory_space=pl.ANY)
SMEM = pl.BlockSpec(memory_space=pltpu.SMEM)
VMEM = pl.BlockSpec(memory_space=pltpu.VMEM)
MIB = 1 << 20


def dot(left, right, dims):
    return lax.dot_general(left, right, (dims, ((), ())), preferred_element_type=F32)


def size_of(axes):
    count = 1
    for name in axes:
        count *= lax.axis_size(name)
    return count


def exchange(blocks, axes):
    return lax.all_to_all(blocks, axes, 0, 0, tiled=True)


def swap(block):
    return lax.ppermute(block, "core", [(0, 1), (1, 0)])


def to_owner(block):
    high, low = lax.axis_size("zh"), lax.axis_size("zl")
    pairs = [(a * high + b, b * low + a) for a in range(low) for b in range(high)]
    return lax.ppermute(block, ("zh", "zl"), pairs)


def call(kernel, outs, operands, later=(), scratch=(), scalars=(), remote=(), weights=(), remote_outs=(), mib=16, flops=0):
    def run(*refs):
        kernel(*refs[: len(operands)], *refs[len(operands) + len(later) :])

    size = sum(o.size * o.dtype.itemsize for o in list(outs) + list(operands))
    return pl.pallas_call(
        run,
        out_shape=outs,
        in_specs=[SMEM if k in scalars else ANY if k in remote or k in weights else VMEM for k in range(len(operands))] + [ANY] * len(later),
        out_specs=[ANY if k in remote_outs else VMEM for k in range(len(outs))],
        scratch_shapes=scratch,
        compiler_params=pltpu.CompilerParams(vmem_limit_bytes=mib * MIB),
        cost_estimate=pl.CostEstimate(flops=flops, bytes_accessed=size, transcendentals=0),
    )(*operands, *later)


def start(source, target, semaphore):
    copy = pltpu.make_async_copy(source, target, semaphore)
    copy.start()
    return copy


def columns(count, width):
    return [slice(k * width, (k + 1) * width) for k in range(count)]


def struct(shape, dtype):
    return jax.ShapeDtypeStruct(shape, dtype)


def split_kernel(inputs_ref, targets_ref, bias_ref, threshold_ref, out_ref, own_ref, sent_ref):
    first = lax.axis_index("core") == 0
    width, half = out_ref.shape[1:]
    block = inputs_ref[...].astype(F32)
    low, high = block[:, :half].astype(BF16), block[:, half:].astype(BF16)
    for k in range(0, out_ref.shape[0], 2):
        out_ref[k] = low
        out_ref[k + 1] = high
    block = targets_ref[...].astype(F32)
    low, high = block[:, :half], block[:, half:]
    own_ref[:width, :half] = jnp.where(first, low, high)
    sent_ref[:width, :half] = jnp.where(first, high, low)
    for ref in (own_ref, sent_ref):
        ref[width : width + 1, :width] = bias_ref[...].astype(F32)
        ref[width + 1 : width + 2, : threshold_ref.shape[1]] = threshold_ref[...]


def column(row):
    return jnp.broadcast_to(row, (8, row.shape[1])).T[:, :1]


def offset_kernel(own_ref, sent_ref, out_ref):
    first = lax.axis_index("core") == 0
    width, half = out_ref.shape
    width //= 2
    own, sent = (
        ref[:width, :half] - column(ref[width : width + 1, :])[:width] for ref in (own_ref, sent_ref)
    )
    out_ref[:width] = jnp.where(first, own, sent)
    out_ref[width:] = jnp.where(first, sent, own)


def flip_kernel(block_ref, out_ref):
    block = block_ref[...].astype(F32).T.astype(BF16)
    for k in range(out_ref.shape[0]):
        out_ref[k] = block


def encode_kernel(
    sizes, blocks_hbm, own_hbm, sent_hbm, own_sides, sent_sides, whole_hbm, code_ref, own_slope, sent_slope,
    blocks, own, sent, whole_ref, sems,
):
    copies = [
        start(blocks_hbm, blocks, sems.at[0]),
        start(own_hbm, own, sems.at[1]),
        start(sent_hbm, sent, sems.at[2]),
    ]
    xs, zh, zl, rest = sizes[:4]
    copies[0].wait()
    for x in range(xs):
        parts = [blocks[x * zl + low, :, high * rest : (high + 1) * rest] for high in range(zh) for low in range(zl)]
        width = len(parts) * rest
        whole_ref[:, x * width : (x + 1) * width] = jnp.concatenate(parts, axis=1)
    out = start(whole_ref, whole_hbm, sems.at[3])
    whole = whole_ref[...]
    codes = []
    weights = ((copies[1], own, own_sides, own_slope), (copies[2], sent, sent_sides, sent_slope))
    for copy, part, sides, slope in weights:
        copy.wait()
        latents = part.shape[0]
        bias = column(sides[sizes[4] + 1 : sizes[4] + 2, :])[:latents]
        shifted = dot(part[...], whole, ((1,), (1,))) - bias
        sig = jax.nn.sigmoid(4.0 * shifted)
        slope[...] = sig + 4.0 * shifted * sig * (1.0 - sig)
        codes.append(shifted * sig)
    code = jnp.concatenate(codes, axis=0).T.astype(BF16)
    for layer in range(code_ref.shape[0]):
        code_ref[layer] = code
    out.wait()


def decode_kernel(codes_ref, own_hbm, sent_hbm, out_hbm, own_ref, sent_ref, out_ref, sems):
    count, _, width = out_ref.shape
    parts = columns(count, width)
    copies = []
    for k, part in enumerate(parts):
        copies.append(start(own_hbm.at[:, part], own_ref.at[:, part], sems.at[0, k]))
        copies.append(start(sent_hbm.at[:, part], sent_ref.at[:, part], sems.at[1, k]))
    section = lax.axis_index("layer")
    layers, _, latents = codes_ref.shape
    latents //= 2
    codes = []
    for layer in range(layers):
        code = codes_ref[layer]
        codes.append(jnp.where(layer <= section, code, jnp.zeros_like(code)))
    own = jnp.concatenate([code[:, :latents] for code in codes], axis=1)
    sent = jnp.concatenate([code[:, latents:] for code in codes], axis=1)
    results = []
    for k, part in enumerate(parts):
        copies[2 * k].wait()
        copies[2 * k + 1].wait()
        total = dot(own, own_ref[:, part], ((1,), (0,))) + dot(sent, sent_ref[:, part], ((1,), (0,)))
        out_ref[k] = total.astype(BF16)
        results.append(start(out_ref.at[k], out_hbm.at[k], sems.at[2, k]))
    for copy in results:
        copy.wait()


def reduce_kernel(rows, parts_hbm, offset_ref, out_ref, parts, sems):
    place = lax.axis_index(FAR)
    copies = [start(parts_hbm.at[k], parts.at[k], sems.at[k]) for k in range(parts.shape[0])]
    size = offset_ref.shape[0]
    tile = jnp.concatenate([offset_ref[...].T] * out_ref.shape[0], axis=1)
    lane = lax.broadcasted_iota(jnp.int32, tile.shape, 1)
    total = jnp.where((lane >= place * size) & (lane < (place + 1) * size), -tile, jnp.zeros_like(tile))
    for k, copy in enumerate(copies):
        copy.wait()
        total += parts[k].astype(F32)
    rest = out_ref.shape[1] - rows
    for k in range(out_ref.shape[0]):
        piece = total[k * rows : (k + 1) * rows]
        if rest > 0:
            piece = jnp.concatenate([piece, jnp.zeros((rest, piece.shape[1]), F32)], axis=0)
        out_ref[k] = piece.astype(BF16)


def error_kernel(rows, scale, positions_ref, parts_ref, out_ref):
    begin = (lax.axis_index("core") * parts_ref.shape[0] + lax.axis_index(FAR)) * rows
    row = lax.broadcasted_iota(jnp.int32, (parts_ref.shape[1], 1), 0)
    mask = jnp.zeros((parts_ref.shape[1], 1), F32)
    for k in range(rows):
        mask = jnp.where(row == k, (positions_ref[begin + k] > 0).astype(F32), mask)
    total = parts_ref[0].astype(F32)
    for k in range(1, parts_ref.shape[0]):
        total += parts_ref[k].astype(F32)
    error = (mask * total * scale).astype(BF16)
    for k in range(out_ref.shape[0]):
        out_ref[k] = error


def repeat_kernel(rows, parts_ref, out_ref):
    parts = [parts_ref[k].astype(F32)[:rows] for k in range(parts_ref.shape[0])]
    block = jnp.concatenate(parts, axis=0).astype(BF16)
    for k in range(out_ref.shape[0]):
        out_ref[k] = block


def back_kernel(error_ref, own_ref, sent_ref, out_ref):
    section = lax.axis_index("layer")
    first = lax.axis_index("core") == 0
    error = jnp.concatenate([error_ref[k] for k in range(error_ref.shape[0])], axis=1)
    own = dot(own_ref[...], error, ((1,), (1,)))
    sent = dot(sent_ref[...], error, ((1,), (1,)))
    latents = out_ref.shape[1]
    for layer in range(out_ref.shape[0] // 2):
        rows = slice(layer * latents, (layer + 1) * latents)
        kept = (layer <= section).astype(F32)
        out_ref[2 * layer] = (jnp.where(first, own[rows], sent[rows]) * kept).astype(BF16)
        out_ref[2 * layer + 1] = (jnp.where(first, sent[rows], own[rows]) * kept).astype(BF16)


def final_kernel(
    terms_ref, own_slope, sent_slope, own_hbm, sent_hbm, grad_hbm, threshold_ref, own_ref, sent_ref, grad_ref, sems
):
    parts = columns(sems.shape[1], own_ref.shape[1] // sems.shape[1])
    copies = []
    for k, part in enumerate(parts):
        copies.append(start(own_hbm.at[:, part], own_ref.at[:, part], sems.at[0, k]))
        copies.append(start(sent_hbm.at[:, part], sent_ref.at[:, part], sems.at[1, k]))
    first = lax.axis_index("core") == 0
    low, high = terms_ref[0].astype(F32), terms_ref[1].astype(F32)
    for k in range(2, terms_ref.shape[0], 2):
        low += terms_ref[k].astype(F32)
        high += terms_ref[k + 1].astype(F32)
    own = jnp.where(first, low, high) * own_slope[...]
    sent = jnp.where(first, high, low) * sent_slope[...]
    total = -jnp.sum(own + sent, axis=1, keepdims=True)
    threshold_ref[...] = jnp.broadcast_to(total, (total.shape[0], 128)).T[:1]
    own, sent = own.astype(BF16), sent.astype(BF16)
    results = []
    for k, part in enumerate(parts):
        copies[2 * k].wait()
        copies[2 * k + 1].wait()
        grad_ref[:, part] = dot(own, own_ref[:, part], ((1,), (0,))) + dot(sent, sent_ref[:, part], ((1,), (0,)))
        results.append(start(grad_ref.at[:, part], grad_hbm.at[:, part], sems.at[2, k]))
    for copy in results:
        copy.wait()


def body(inputs, targets, encoder, threshold, decoders, out_bias, positions):
    layers = lax.axis_size("layer")
    width, tokens = inputs.shape[2], inputs.shape[1]
    half = tokens // 2
    latents, model = encoder.shape[1], encoder.shape[2]
    xs, zh, zl, yh = (lax.axis_size(name) for name in ("x", "zh", "zl", "yh"))
    near, far = xs * zl, zh * yh
    wide, rows = model // near, half // far
    tall = -(-rows // 16) * 16

    side = struct((width + 8, 128), F32)
    sends, own_sides, sent_sides = call(
        split_kernel,
        [struct((2 * far, width, half), BF16), side, side],
        [inputs[0].T, targets[0].T, out_bias, threshold],
    )
    block = exchange(sends, FAR + ("core",)).reshape(-1, half)
    own_encoder = encoder[0]
    own_decoders = decoders[0].reshape(layers * latents, model)
    held = (block, own_encoder, own_decoders, sent_sides)
    block, sent_encoder, sent_decoders, sent_sides = lax.optimization_barrier(held)
    other_sides = swap(sent_sides)
    other_encoder = swap(sent_encoder)
    other_decoders = swap(sent_decoders)
    (sends,) = call(flip_kernel, [struct((near, half, wide), BF16)], [block])
    blocks = exchange(sends, NEAR)
    whole, codes, own_slope, sent_slope = call(
        functools.partial(encode_kernel, (xs, zh, zl, wide // zh, width)),
        [
            struct((half, model), BF16),
            struct((layers, half, 2 * latents), BF16),
            struct((latents, half), F32),
            struct((latents, half), F32),
        ],
        [blocks, own_encoder, other_encoder, own_sides, other_sides],
        scratch=[
            pltpu.VMEM((near, half, wide), BF16),
            pltpu.VMEM((latents, model), BF16),
            pltpu.VMEM((latents, model), BF16),
            pltpu.VMEM((half, model), BF16),
            pltpu.SemaphoreType.DMA((4,)),
        ],
        remote=[0],
        weights=[1, 2],
        remote_outs=[0],
        flops=4 * half * latents * model,
    )
    codes = exchange(codes, ("layer",))
    (offset,) = call(offset_kernel, [struct((2 * width, half), F32)], [own_sides, other_sides])
    offset = to_owner(offset)
    other_whole = swap(whole)
    other_slope = swap(sent_slope)

    (parts,) = call(
        decode_kernel,
        [struct((near, half, wide), BF16)],
        [codes, own_decoders, other_decoders],
        scratch=[
            pltpu.VMEM((layers * latents, model), BF16),
            pltpu.VMEM((layers * latents, model), BF16),
            pltpu.VMEM((near, half, wide), BF16),
            pltpu.SemaphoreType.DMA((3, near)),
        ],
        weights=[1, 2],
        remote_outs=[0],
        mib=62,
        flops=4 * layers * half * latents * model,
    )
    parts = exchange(parts, NEAR)
    parts, offset, other_whole, other_slope = lax.optimization_barrier((parts, offset, other_whole, other_slope))
    (parts,) = call(
        functools.partial(reduce_kernel, rows),
        [struct((far, tall, wide), BF16)],
        [parts, offset],
        scratch=[pltpu.VMEM((near, half, wide), BF16), pltpu.SemaphoreType.DMA((near,))],
        remote=[0],
    )
    parts = exchange(parts, FAR)
    (parts,) = call(
        functools.partial(error_kernel, rows, 1.0 / layers),
        [struct((far, tall, wide), BF16)],
        [positions, parts],
        scalars=[0],
    )
    parts = exchange(parts, FAR)
    (parts,) = call(functools.partial(repeat_kernel, rows), [struct((near, half, wide), BF16)], [parts])
    error = exchange(parts, NEAR)
    (terms,) = call(
        back_kernel,
        [struct((2 * layers, latents, half), BF16)],
        [error, own_decoders, other_decoders],
        flops=4 * layers * half * latents * model,
    )
    terms = exchange(terms, ("layer", "core"))
    grad_encoder, grad_threshold = call(
        final_kernel,
        [struct((latents, model), F32), struct((1, latents), F32)],
        [terms, own_slope, other_slope, whole, other_whole],
        scratch=[
            pltpu.VMEM((half, model), BF16),
            pltpu.VMEM((half, model), BF16),
            pltpu.VMEM((latents, model), F32),
            pltpu.SemaphoreType.DMA((3, 4)),
        ],
        weights=[3, 4],
        remote_outs=[0],
        flops=4 * half * latents * model,
    )
    return (grad_encoder[None], grad_threshold)


LATENT = ("x", "zh", "zl", "yh", "core")


def solution(mesh, parts=(4, 4, 2, 2, 2)):
    in_specs = (
        P("layer", None, LATENT),
        P("layer", None, LATENT),
        P("layer", LATENT, None),
        P("layer", LATENT),
        P("layer", None, LATENT, None),
        P("layer", LATENT),
        P(),
    )
    out_specs = (P("layer", LATENT, None), P("layer", LATENT))
    devices = mesh.devices.reshape((mesh.devices.shape[0],) + parts)
    fine = Mesh(devices, ("layer",) + LATENT)
    return jax.shard_map(body, mesh=fine, in_specs=in_specs, out_specs=out_specs, check_vma=False)
```

```python
import functools

import jax
import jax.numpy as jnp
from jax import lax
from jax.experimental import pallas as pl
from jax.experimental.pallas import tpu as pltpu
from jax.sharding import Mesh, PartitionSpec as P

F32 = jnp.float32
BF16 = jnp.bfloat16
NEAR = ("x", "zl")
FAR = ("zh", "yh")
ANY = pl.BlockSpec(memory_space=pl.ANY)
VMEM = pl.BlockSpec(memory_space=pltpu.VMEM)
MIB = 1 << 20


def dot(left, right, dims):
    return lax.dot_general(left, right, (dims, ((), ())), preferred_element_type=F32)


def size_of(axes):
    count = 1
    for name in axes:
        count *= lax.axis_size(name)
    return count


def exchange(blocks, axes):
    return lax.all_to_all(blocks, axes, 0, 0, tiled=True)


def swap(block):
    return lax.ppermute(block, "core", [(0, 1), (1, 0)])


def to_owner(block):
    high, low = lax.axis_size("zh"), lax.axis_size("zl")
    pairs = [(a * high + b, b * low + a) for a in range(low) for b in range(high)]
    return lax.ppermute(block, ("zh", "zl"), pairs)


def call(kernel, outs, operands, later=(), scratch=(), remote=(), remote_outs=(), mib=16, flops=0):
    def run(*refs):
        kernel(*refs[: len(operands)], *refs[len(operands) + len(later) :])

    size = sum(o.size * o.dtype.itemsize for o in list(outs) + list(operands))
    return pl.pallas_call(
        run,
        out_shape=outs,
        in_specs=[ANY if k in remote else VMEM for k in range(len(operands))] + [ANY] * len(later),
        out_specs=[ANY if k in remote_outs else VMEM for k in range(len(outs))],
        scratch_shapes=scratch,
        compiler_params=pltpu.CompilerParams(vmem_limit_bytes=mib * MIB),
        cost_estimate=pl.CostEstimate(flops=flops, bytes_accessed=size, transcendentals=0),
    )(*operands, *later)


def start(source, target, semaphore):
    copy = pltpu.make_async_copy(source, target, semaphore)
    copy.start()
    return copy


def columns(count, width):
    return [slice(k * width, (k + 1) * width) for k in range(count)]


def struct(shape, dtype):
    return jax.ShapeDtypeStruct(shape, dtype)


def split_kernel(inputs_ref, targets_ref, bias_ref, threshold_ref, out_ref, own_ref, sent_ref):
    first = lax.axis_index("core") == 0
    width, half = out_ref.shape[1:]
    block = inputs_ref[...].astype(F32)
    low, high = block[:, :half].astype(BF16), block[:, half:].astype(BF16)
    for k in range(0, out_ref.shape[0], 2):
        out_ref[k] = low
        out_ref[k + 1] = high
    block = targets_ref[...].astype(F32)
    low, high = block[:, :half], block[:, half:]
    own_ref[:width, :half] = jnp.where(first, low, high)
    sent_ref[:width, :half] = jnp.where(first, high, low)
    for ref in (own_ref, sent_ref):
        ref[width : width + 1, :width] = bias_ref[...].astype(F32)
        ref[width + 1 : width + 2, : threshold_ref.shape[1]] = threshold_ref[...]


def column(row):
    return jnp.broadcast_to(row, (8, row.shape[1])).T[:, :1]


def offset_kernel(own_ref, sent_ref, out_ref):
    first = lax.axis_index("core") == 0
    width, half = out_ref.shape
    width //= 2
    own, sent = (
        ref[:width, :half] - column(ref[width : width + 1, :])[:width] for ref in (own_ref, sent_ref)
    )
    out_ref[:width] = jnp.where(first, own, sent)
    out_ref[width:] = jnp.where(first, sent, own)


def flip_kernel(block_ref, out_ref):
    block = block_ref[...].astype(F32).T.astype(BF16)
    for k in range(out_ref.shape[0]):
        out_ref[k] = block


def encode_kernel(
    sizes, blocks_ref, own_hbm, sent_hbm, own_sides, sent_sides, whole_hbm, code_ref, own_slope, sent_slope,
    weights, whole_ref, sems,
):
    xs, zh, zl, rest, width = sizes
    latents = own_slope.shape[0]
    copies = [
        start(own_hbm, weights.at[:latents], sems.at[0]),
        start(sent_hbm, weights.at[latents:], sems.at[1]),
    ]
    for x in range(xs):
        parts = [blocks_ref[x * zl + low, :, high * rest : (high + 1) * rest] for high in range(zh) for low in range(zl)]
        size = len(parts) * rest
        whole_ref[:, x * size : (x + 1) * size] = jnp.concatenate(parts, axis=1)
    out = start(whole_ref, whole_hbm, sems.at[2])
    for copy in copies:
        copy.wait()
    bias = [column(sides[width + 1 : width + 2, :])[:latents] for sides in (own_sides, sent_sides)]
    shifted = dot(weights[...], whole_ref[...], ((1,), (1,))) - jnp.concatenate(bias, axis=0)
    sig = jax.nn.sigmoid(4.0 * shifted)
    slope = sig + 4.0 * shifted * sig * (1.0 - sig)
    own_slope[...] = slope[:latents]
    sent_slope[...] = slope[latents:]
    code = (shifted * sig).T.astype(BF16)
    for layer in range(code_ref.shape[0]):
        code_ref[layer] = code
    out.wait()


def decode_kernel(codes_ref, own_hbm, sent_hbm, out_hbm, own_ref, sent_ref, total_ref, out_ref, sems):
    layers, _, latents = codes_ref.shape
    latents //= 2
    copies = []
    for k, (source, target) in enumerate(((own_hbm, own_ref), (sent_hbm, sent_ref))):
        for layer in range(layers):
            rows = slice(layer * latents, (layer + 1) * latents)
            copies.append(start(source.at[rows], target.at[rows], sems.at[k, layer]))
    section = lax.axis_index("layer")
    codes = []
    for layer in range(layers):
        code = codes_ref[layer]
        codes.append(jnp.where(layer <= section, code, jnp.zeros_like(code)))
    own = jnp.concatenate([code[:, :latents] for code in codes], axis=1)
    sent = jnp.concatenate([code[:, latents:] for code in codes], axis=1)
    parts = columns(out_ref.shape[0], out_ref.shape[2])
    for copy in copies[:layers]:
        copy.wait()
    for k, part in enumerate(parts):
        total_ref[k] = dot(own, own_ref[:, part], ((1,), (0,)))
    for copy in copies[layers:]:
        copy.wait()
    results = []
    for k, part in enumerate(parts):
        out_ref[k] = (total_ref[k] + dot(sent, sent_ref[:, part], ((1,), (0,)))).astype(BF16)
        results.append(start(out_ref.at[k], out_hbm.at[k], sems.at[2, k]))
    for copy in results:
        copy.wait()


def reduce_kernel(parts_hbm, offset_ref, out_ref, parts, sems):
    place = lax.axis_index(FAR)
    copies = [start(parts_hbm.at[k], parts.at[k], sems.at[k]) for k in range(parts.shape[0])]
    size = offset_ref.shape[0]
    tile = jnp.concatenate([offset_ref[...].T] * (parts.shape[2] // size), axis=1)
    lane = lax.broadcasted_iota(jnp.int32, tile.shape, 1)
    total = jnp.where((lane >= place * size) & (lane < (place + 1) * size), -tile, jnp.zeros_like(tile))
    for k, copy in enumerate(copies):
        copy.wait()
        total += parts[k].astype(F32)
    total = total.astype(BF16)
    for k in range(out_ref.shape[0]):
        out_ref[k] = total


def error_kernel(scale, positions_ref, parts_ref, out_ref):
    half = parts_ref.shape[1]
    token_mask = (positions_ref[...] > 0).astype(F32)
    mask = jnp.where(lax.axis_index("core") == 0, token_mask[:, :half], token_mask[:, half:])
    total = parts_ref[0].astype(F32)
    for k in range(1, parts_ref.shape[0]):
        total += parts_ref[k].astype(F32)
    error = (column(mask) * total * scale).astype(BF16)
    for k in range(out_ref.shape[0]):
        out_ref[k] = error


def back_kernel(error_ref, own_ref, sent_ref, out_ref):
    section = lax.axis_index("layer")
    first = lax.axis_index("core") == 0
    error = jnp.concatenate([error_ref[k] for k in range(error_ref.shape[0])], axis=1)
    own = dot(own_ref[...], error, ((1,), (1,)))
    sent = dot(sent_ref[...], error, ((1,), (1,)))
    latents = out_ref.shape[1]
    for layer in range(out_ref.shape[0] // 2):
        rows = slice(layer * latents, (layer + 1) * latents)
        kept = (layer <= section).astype(F32)
        out_ref[2 * layer] = (jnp.where(first, own[rows], sent[rows]) * kept).astype(BF16)
        out_ref[2 * layer + 1] = (jnp.where(first, sent[rows], own[rows]) * kept).astype(BF16)


def final_kernel(terms_ref, own_slope, sent_slope, own_ref, sent_ref, grad_hbm, threshold_ref, grad_ref, sems):
    first = lax.axis_index("core") == 0
    low, high = terms_ref[0].astype(F32), terms_ref[1].astype(F32)
    for k in range(2, terms_ref.shape[0], 2):
        low += terms_ref[k].astype(F32)
        high += terms_ref[k + 1].astype(F32)
    own = jnp.where(first, low, high) * own_slope[...]
    sent = jnp.where(first, high, low) * sent_slope[...]
    lows, highs = own.astype(BF16), sent.astype(BF16)
    results = []
    for k, part in enumerate(columns(sems.shape[0], own_ref.shape[1] // sems.shape[0])):
        grad_ref[:, part] = dot(lows, own_ref[:, part], ((1,), (0,))) + dot(highs, sent_ref[:, part], ((1,), (0,)))
        results.append(start(grad_ref.at[:, part], grad_hbm.at[:, part], sems.at[k]))
    total = -jnp.sum(own + sent, axis=1, keepdims=True)
    threshold_ref[...] = jnp.broadcast_to(total, (total.shape[0], 128)).T[:1]
    for copy in results:
        copy.wait()


def body(inputs, targets, encoder, threshold, decoders, out_bias, positions):
    layers = lax.axis_size("layer")
    width, tokens = inputs.shape[2], inputs.shape[1]
    half = tokens // 2
    latents, model = encoder.shape[1], encoder.shape[2]
    xs, zh, zl, yh = (lax.axis_size(name) for name in ("x", "zh", "zl", "yh"))
    near, far = xs * zl, zh * yh
    wide = model // near

    side = struct((width + 8, 128), F32)
    sends, own_sides, sent_sides = call(
        split_kernel,
        [struct((2 * far, width, half), BF16), side, side],
        [inputs[0].T, targets[0].T, out_bias, threshold],
        mib=62,
    )
    own_encoder = encoder[0]
    own_decoders = decoders[0].reshape(layers * latents, model)
    own_encoder = encoder[0]
    sends, own_decoders = lax.optimization_barrier((sends, decoders[0]))
    other_decoders = [swap(own_decoders[layer]) for layer in range(layers)]
    own_decoders = own_decoders.reshape(layers * latents, model)
    block = exchange(sends, FAR + ("core",)).reshape(-1, half)
    held = (block, own_encoder, own_decoders, sent_sides)
    block, sent_encoder, sent_decoders, sent_sides = lax.optimization_barrier(held)
    other_sides = swap(sent_sides)
    other_encoder = swap(sent_encoder)
    other_decoders = swap(sent_decoders)
    (sends,) = call(flip_kernel, [struct((near, half, wide), BF16)], [block])
    blocks = exchange(sends, NEAR)
    whole, codes, own_slope, sent_slope = call(
        functools.partial(encode_kernel, (xs, zh, zl, wide // zh, width)),
        [
            struct((half, model), BF16),
            struct((layers, half, 2 * latents), BF16),
            struct((latents, half), F32),
            struct((latents, half), F32),
        ],
        [blocks, own_encoder, other_encoder, own_sides, other_sides],
        scratch=[
            pltpu.VMEM((2 * latents, model), BF16),
            pltpu.VMEM((half, model), BF16),
            pltpu.SemaphoreType.DMA((3,)),
        ],
        remote=[1, 2],
        remote_outs=[0],
        flops=4 * half * latents * model,
    )
    codes = exchange(codes, ("layer",))
    (offset,) = call(offset_kernel, [struct((2 * width, half), F32)], [own_sides, other_sides])
    offset = to_owner(offset)
    other_whole = swap(whole)
    other_slope = swap(sent_slope)

    (parts,) = call(
        decode_kernel,
        [struct((near, half, wide), BF16)],
        [codes, own_decoders, other_decoders],
        scratch=[
            pltpu.VMEM((layers * latents, model), BF16),
            pltpu.VMEM((layers * latents, model), BF16),
            pltpu.VMEM((near, half, wide), F32),
            pltpu.VMEM((near, half, wide), BF16),
            pltpu.SemaphoreType.DMA((3, near)),
        ],
        remote=[1, 2],
        remote_outs=[0],
        mib=62,
        flops=4 * layers * half * latents * model,
    )
    parts = exchange(parts, NEAR)
    parts, offset, other_whole, other_slope = lax.optimization_barrier((parts, offset, other_whole, other_slope))
    (parts,) = call(
        reduce_kernel,
        [struct((far, half, wide), BF16)],
        [parts, offset],
        scratch=[pltpu.VMEM((near, half, wide), BF16), pltpu.SemaphoreType.DMA((near,))],
        remote=[0],
    )
    parts = exchange(parts, FAR)
    (parts,) = call(
        functools.partial(error_kernel, 1.0 / layers), [struct((near, half, wide), BF16)], [positions[None], parts]
    )
    error = exchange(parts, NEAR)
    (terms,) = call(
        back_kernel,
        [struct((2 * layers, latents, half), BF16)],
        [error, own_decoders, other_decoders],
        flops=4 * layers * half * latents * model,
    )
    terms = exchange(terms, ("layer", "core"))
    grad_encoder, grad_threshold = call(
        final_kernel,
        [struct((latents, model), F32), struct((1, latents), F32)],
        [terms, own_slope, other_slope, whole, other_whole],
        scratch=[pltpu.VMEM((latents, model), F32), pltpu.SemaphoreType.DMA((8,))],
        remote_outs=[0],
        flops=4 * half * latents * model,
    )
    return (grad_encoder[None], grad_threshold)


LATENT = ("x", "zh", "zl", "yh", "core")


def solution(mesh, parts=(4, 4, 2, 2, 2)):
    in_specs = (
        P("layer", None, LATENT),
        P("layer", None, LATENT),
        P("layer", LATENT, None),
        P("layer", LATENT),
        P("layer", None, LATENT, None),
        P("layer", LATENT),
        P(),
    )
    out_specs = (P("layer", LATENT, None), P("layer", LATENT))
    devices = mesh.devices.reshape((mesh.devices.shape[0],) + parts)
    fine = Mesh(devices, ("layer",) + LATENT)
    return jax.shard_map(body, mesh=fine, in_specs=in_specs, out_specs=out_specs, check_vma=False)
```

```python
import functools

import jax
import jax.numpy as jnp
from jax import lax
from jax.experimental import pallas as pl
from jax.experimental.pallas import tpu as pltpu
from jax.sharding import Mesh, PartitionSpec as P

F32 = jnp.float32
BF16 = jnp.bfloat16
NEAR = ("x", "zl")
FAR = ("zh", "yh")
ANY = pl.BlockSpec(memory_space=pl.ANY)
VMEM = pl.BlockSpec(memory_space=pltpu.VMEM)
MIB = 1 << 20


def dot(left, right, dims):
    return lax.dot_general(left, right, (dims, ((), ())), preferred_element_type=F32)


def size_of(axes):
    count = 1
    for name in axes:
        count *= lax.axis_size(name)
    return count


def exchange(blocks, axes):
    return lax.all_to_all(blocks, axes, 0, 0, tiled=True)


def swap(block):
    return lax.ppermute(block, "core", [(0, 1), (1, 0)])


def to_owner(block):
    high, low = lax.axis_size("zh"), lax.axis_size("zl")
    pairs = [(a * high + b, b * low + a) for a in range(low) for b in range(high)]
    return lax.ppermute(block, ("zh", "zl"), pairs)


def call(kernel, outs, operands, later=(), scratch=(), remote=(), remote_outs=(), mib=16, flops=0):
    def run(*refs):
        kernel(*refs[: len(operands)], *refs[len(operands) + len(later) :])

    size = sum(o.size * o.dtype.itemsize for o in list(outs) + list(operands))
    return pl.pallas_call(
        run,
        out_shape=outs,
        in_specs=[ANY if k in remote else VMEM for k in range(len(operands))] + [ANY] * len(later),
        out_specs=[ANY if k in remote_outs else VMEM for k in range(len(outs))],
        scratch_shapes=scratch,
        compiler_params=pltpu.CompilerParams(vmem_limit_bytes=mib * MIB),
        cost_estimate=pl.CostEstimate(flops=flops, bytes_accessed=size, transcendentals=0),
    )(*operands, *later)


def start(source, target, semaphore):
    copy = pltpu.make_async_copy(source, target, semaphore)
    copy.start()
    return copy


def columns(count, width):
    return [slice(k * width, (k + 1) * width) for k in range(count)]


def struct(shape, dtype):
    return jax.ShapeDtypeStruct(shape, dtype)


def split_kernel(inputs_ref, targets_ref, bias_ref, threshold_ref, out_ref, own_ref, sent_ref):
    first = lax.axis_index("core") == 0
    width, half = out_ref.shape[1:]
    block = inputs_ref[...].astype(F32)
    low, high = block[:, :half].astype(BF16), block[:, half:].astype(BF16)
    for k in range(0, out_ref.shape[0], 2):
        out_ref[k] = low
        out_ref[k + 1] = high
    block = targets_ref[...].astype(F32)
    low, high = block[:, :half], block[:, half:]
    own_ref[:width, :half] = jnp.where(first, low, high)
    sent_ref[:width, :half] = jnp.where(first, high, low)
    for ref in (own_ref, sent_ref):
        ref[width : width + 1, :width] = bias_ref[...].astype(F32)
        ref[width + 1 : width + 2, : threshold_ref.shape[1]] = threshold_ref[...]


def column(row):
    return jnp.broadcast_to(row, (8, row.shape[1])).T[:, :1]


def offset_kernel(own_ref, sent_ref, out_ref):
    first = lax.axis_index("core") == 0
    width, half = out_ref.shape
    width //= 2
    own, sent = (
        ref[:width, :half] - column(ref[width : width + 1, :])[:width] for ref in (own_ref, sent_ref)
    )
    out_ref[:width] = jnp.where(first, own, sent)
    out_ref[width:] = jnp.where(first, sent, own)


def flip_kernel(block_ref, out_ref):
    block = block_ref[...].astype(F32).T.astype(BF16)
    for k in range(out_ref.shape[0]):
        out_ref[k] = block


def encode_kernel(
    sizes, blocks_ref, own_hbm, sent_hbm, own_sides, sent_sides, whole_hbm, code_ref, own_slope, sent_slope,
    weights, whole_ref, sems,
):
    xs, zh, zl, rest, width = sizes
    latents = own_slope.shape[0]
    copies = [
        start(own_hbm, weights.at[:latents], sems.at[0]),
        start(sent_hbm, weights.at[latents:], sems.at[1]),
    ]
    for x in range(xs):
        parts = [blocks_ref[x * zl + low, :, high * rest : (high + 1) * rest] for high in range(zh) for low in range(zl)]
        size = len(parts) * rest
        whole_ref[:, x * size : (x + 1) * size] = jnp.concatenate(parts, axis=1)
    out = start(whole_ref, whole_hbm, sems.at[2])
    for copy in copies:
        copy.wait()
    bias = [column(sides[width + 1 : width + 2, :])[:latents] for sides in (own_sides, sent_sides)]
    shifted = dot(weights[...], whole_ref[...], ((1,), (1,))) - jnp.concatenate(bias, axis=0)
    sig = jax.nn.sigmoid(4.0 * shifted)
    slope = sig + 4.0 * shifted * sig * (1.0 - sig)
    own_slope[...] = slope[:latents]
    sent_slope[...] = slope[latents:]
    code = (shifted * sig).T.astype(BF16)
    for layer in range(code_ref.shape[0]):
        code_ref[layer] = code
    out.wait()


def decode_kernel(codes_ref, own_hbm, sent_hbm, out_hbm, own_ref, sent_ref, total_ref, out_ref, sems):
    layers, _, latents = codes_ref.shape
    latents //= 2
    copies = []
    for k, (source, target) in enumerate(((own_hbm, own_ref), (sent_hbm, sent_ref))):
        for layer in range(layers):
            rows = slice(layer * latents, (layer + 1) * latents)
            copies.append(start(source.at[rows], target.at[rows], sems.at[k, layer]))
    section = lax.axis_index("layer")
    codes = []
    for layer in range(layers):
        code = codes_ref[layer]
        codes.append(jnp.where(layer <= section, code, jnp.zeros_like(code)))
    own = jnp.concatenate([code[:, :latents] for code in codes], axis=1)
    sent = jnp.concatenate([code[:, latents:] for code in codes], axis=1)
    parts = columns(out_ref.shape[0], out_ref.shape[2])
    for copy in copies[:layers]:
        copy.wait()
    for k, part in enumerate(parts):
        total_ref[k] = dot(own, own_ref[:, part], ((1,), (0,)))
    for copy in copies[layers:]:
        copy.wait()
    results = []
    for k, part in enumerate(parts):
        out_ref[k] = (total_ref[k] + dot(sent, sent_ref[:, part], ((1,), (0,)))).astype(BF16)
        results.append(start(out_ref.at[k], out_hbm.at[k], sems.at[2, k]))
    for copy in results:
        copy.wait()


def reduce_kernel(parts_hbm, offset_ref, out_ref, parts, sems):
    place = lax.axis_index(FAR)
    copies = [start(parts_hbm.at[k], parts.at[k], sems.at[k]) for k in range(parts.shape[0])]
    size = offset_ref.shape[0]
    tile = jnp.concatenate([offset_ref[...].T] * (parts.shape[2] // size), axis=1)
    lane = lax.broadcasted_iota(jnp.int32, tile.shape, 1)
    total = jnp.where((lane >= place * size) & (lane < (place + 1) * size), -tile, jnp.zeros_like(tile))
    for k, copy in enumerate(copies):
        copy.wait()
        total += parts[k].astype(F32)
    rows = out_ref.shape[1]
    for k in range(out_ref.shape[0]):
        out_ref[k] = total[k * rows : (k + 1) * rows]


def sum_kernel(parts_ref, out_ref):
    total = parts_ref[0]
    for k in range(1, parts_ref.shape[0]):
        total += parts_ref[k]
    total = total.astype(BF16)
    for k in range(out_ref.shape[0]):
        out_ref[k] = total


def error_kernel(pair, scale, positions_ref, parts_ref, out_ref):
    half = out_ref.shape[1]
    token_mask = (positions_ref[...] > 0).astype(F32)
    mask = jnp.where(lax.axis_index("core") == 0, token_mask[:, :half], token_mask[:, half:])
    totals = []
    for k in range(0, parts_ref.shape[0], pair):
        total = parts_ref[k].astype(F32)
        for j in range(k + 1, k + pair):
            total += parts_ref[j].astype(F32)
        totals.append(total)
    error = (column(mask) * jnp.concatenate(totals, axis=0) * scale).astype(BF16)
    for k in range(out_ref.shape[0]):
        out_ref[k] = error


def back_kernel(error_ref, own_ref, sent_ref, out_ref):
    section = lax.axis_index("layer")
    first = lax.axis_index("core") == 0
    error = jnp.concatenate([error_ref[k] for k in range(error_ref.shape[0])], axis=1)
    own = dot(own_ref[...], error, ((1,), (1,)))
    sent = dot(sent_ref[...], error, ((1,), (1,)))
    latents = out_ref.shape[1]
    for layer in range(out_ref.shape[0] // 2):
        rows = slice(layer * latents, (layer + 1) * latents)
        kept = (layer <= section).astype(F32)
        out_ref[2 * layer] = (jnp.where(first, own[rows], sent[rows]) * kept).astype(BF16)
        out_ref[2 * layer + 1] = (jnp.where(first, sent[rows], own[rows]) * kept).astype(BF16)


def final_kernel(terms_ref, own_slope, sent_slope, own_ref, sent_ref, grad_hbm, threshold_ref, grad_ref, sems):
    first = lax.axis_index("core") == 0
    low, high = terms_ref[0].astype(F32), terms_ref[1].astype(F32)
    for k in range(2, terms_ref.shape[0], 2):
        low += terms_ref[k].astype(F32)
        high += terms_ref[k + 1].astype(F32)
    own = jnp.where(first, low, high) * own_slope[...]
    sent = jnp.where(first, high, low) * sent_slope[...]
    lows, highs = own.astype(BF16), sent.astype(BF16)
    results = []
    for k, part in enumerate(columns(sems.shape[0], own_ref.shape[1] // sems.shape[0])):
        grad_ref[:, part] = dot(lows, own_ref[:, part], ((1,), (0,))) + dot(highs, sent_ref[:, part], ((1,), (0,)))
        results.append(start(grad_ref.at[:, part], grad_hbm.at[:, part], sems.at[k]))
    total = -jnp.sum(own + sent, axis=1, keepdims=True)
    threshold_ref[...] = jnp.broadcast_to(total, (total.shape[0], 128)).T[:1]
    for copy in results:
        copy.wait()


def body(inputs, targets, encoder, threshold, decoders, out_bias, positions):
    layers = lax.axis_size("layer")
    width, tokens = inputs.shape[2], inputs.shape[1]
    half = tokens // 2
    latents, model = encoder.shape[1], encoder.shape[2]
    xs, zh, zl, yh = (lax.axis_size(name) for name in ("x", "zh", "zl", "yh"))
    near, far = xs * zl, zh * yh
    wide = model // near

    side = struct((width + 8, 128), F32)
    sends, own_sides, sent_sides = call(
        split_kernel,
        [struct((2 * far, width, half), BF16), side, side],
        [inputs[0].T, targets[0].T, out_bias, threshold],
        mib=62,
    )
    own_encoder = encoder[0]
    own_decoders = decoders[0].reshape(layers * latents, model)
    own_encoder = encoder[0]
    sends, own_decoders = lax.optimization_barrier((sends, decoders[0]))
    other_decoders = [swap(own_decoders[layer]) for layer in range(layers)]
    own_decoders = own_decoders.reshape(layers * latents, model)
    block = exchange(sends, FAR + ("core",)).reshape(-1, half)
    held = (block, own_encoder, own_decoders, sent_sides)
    block, sent_encoder, sent_decoders, sent_sides = lax.optimization_barrier(held)
    other_sides = swap(sent_sides)
    other_encoder = swap(sent_encoder)
    other_decoders = swap(sent_decoders)
    (sends,) = call(flip_kernel, [struct((near, half, wide), BF16)], [block])
    blocks = exchange(sends, NEAR)
    whole, codes, own_slope, sent_slope = call(
        functools.partial(encode_kernel, (xs, zh, zl, wide // zh, width)),
        [
            struct((half, model), BF16),
            struct((layers, half, 2 * latents), BF16),
            struct((latents, half), F32),
            struct((latents, half), F32),
        ],
        [blocks, own_encoder, other_encoder, own_sides, other_sides],
        scratch=[
            pltpu.VMEM((2 * latents, model), BF16),
            pltpu.VMEM((half, model), BF16),
            pltpu.SemaphoreType.DMA((3,)),
        ],
        remote=[1, 2],
        remote_outs=[0],
        flops=4 * half * latents * model,
    )
    codes = exchange(codes, ("layer",))
    (offset,) = call(offset_kernel, [struct((2 * width, half), F32)], [own_sides, other_sides])
    offset = to_owner(offset)
    other_whole = swap(whole)
    other_slope = swap(sent_slope)

    (parts,) = call(
        decode_kernel,
        [struct((near, half, wide), BF16)],
        [codes, own_decoders, other_decoders],
        scratch=[
            pltpu.VMEM((layers * latents, model), BF16),
            pltpu.VMEM((layers * latents, model), BF16),
            pltpu.VMEM((near, half, wide), F32),
            pltpu.VMEM((near, half, wide), BF16),
            pltpu.SemaphoreType.DMA((3, near)),
        ],
        remote=[1, 2],
        remote_outs=[0],
        mib=62,
        flops=4 * layers * half * latents * model,
    )
    parts = exchange(parts, NEAR)
    parts, offset, other_whole, other_slope = lax.optimization_barrier((parts, offset, other_whole, other_slope))
    (parts,) = call(
        reduce_kernel,
        [struct((zh, half // zh, wide), F32)],
        [parts, offset],
        scratch=[pltpu.VMEM((near, half, wide), BF16), pltpu.SemaphoreType.DMA((near,))],
        remote=[0],
    )
    parts = exchange(parts, ("zh",))
    (parts,) = call(sum_kernel, [struct((far, half // zh, wide), BF16)], [parts])
    parts = exchange(parts, FAR)
    (parts,) = call(
        functools.partial(error_kernel, yh, 1.0 / layers),
        [struct((near, half, wide), BF16)],
        [positions[None], parts],
    )
    error = exchange(parts, NEAR)
    (terms,) = call(
        back_kernel,
        [struct((2 * layers, latents, half), BF16)],
        [error, own_decoders, other_decoders],
        flops=4 * layers * half * latents * model,
    )
    terms = exchange(terms, ("layer", "core"))
    grad_encoder, grad_threshold = call(
        final_kernel,
        [struct((latents, model), F32), struct((1, latents), F32)],
        [terms, own_slope, other_slope, whole, other_whole],
        scratch=[pltpu.VMEM((latents, model), F32), pltpu.SemaphoreType.DMA((8,))],
        remote_outs=[0],
        flops=4 * half * latents * model,
    )
    return (grad_encoder[None], grad_threshold)


LATENT = ("x", "zh", "zl", "yh", "core")


def solution(mesh, parts=(4, 4, 2, 2, 2)):
    in_specs = (
        P("layer", None, LATENT),
        P("layer", None, LATENT),
        P("layer", LATENT, None),
        P("layer", LATENT),
        P("layer", None, LATENT, None),
        P("layer", LATENT),
        P(),
    )
    out_specs = (P("layer", LATENT, None), P("layer", LATENT))
    devices = mesh.devices.reshape((mesh.devices.shape[0],) + parts)
    fine = Mesh(devices, ("layer",) + LATENT)
    return jax.shard_map(body, mesh=fine, in_specs=in_specs, out_specs=out_specs, check_vma=False)
```

```python
import functools

import jax
import jax.numpy as jnp
from jax import lax
from jax.experimental import pallas as pl
from jax.experimental.pallas import tpu as pltpu
from jax.sharding import Mesh, PartitionSpec as P

F32 = jnp.float32
BF16 = jnp.bfloat16
NEAR = ("x", "zl")
FAR = ("zh", "yh")
ANY = pl.BlockSpec(memory_space=pl.ANY)
VMEM = pl.BlockSpec(memory_space=pltpu.VMEM)
MIB = 1 << 20


def dot(left, right, dims):
    return lax.dot_general(left, right, (dims, ((), ())), preferred_element_type=F32)


def size_of(axes):
    count = 1
    for name in axes:
        count *= lax.axis_size(name)
    return count


def exchange(blocks, axes):
    return lax.all_to_all(blocks, axes, 0, 0, tiled=True)


def swap(block):
    return lax.ppermute(block, "core", [(0, 1), (1, 0)])


def to_owner(block):
    high, low = lax.axis_size("zh"), lax.axis_size("zl")
    pairs = [(a * high + b, b * low + a) for a in range(low) for b in range(high)]
    return lax.ppermute(block, ("zh", "zl"), pairs)


def call(kernel, outs, operands, later=(), scratch=(), remote=(), remote_outs=(), mib=16, flops=0):
    def run(*refs):
        kernel(*refs[: len(operands)], *refs[len(operands) + len(later) :])

    size = sum(o.size * o.dtype.itemsize for o in list(outs) + list(operands))
    return pl.pallas_call(
        run,
        out_shape=outs,
        in_specs=[ANY if k in remote else VMEM for k in range(len(operands))] + [ANY] * len(later),
        out_specs=[ANY if k in remote_outs else VMEM for k in range(len(outs))],
        scratch_shapes=scratch,
        compiler_params=pltpu.CompilerParams(vmem_limit_bytes=mib * MIB),
        cost_estimate=pl.CostEstimate(flops=flops, bytes_accessed=size, transcendentals=0),
    )(*operands, *later)


def start(source, target, semaphore):
    copy = pltpu.make_async_copy(source, target, semaphore)
    copy.start()
    return copy


def columns(count, width):
    return [slice(k * width, (k + 1) * width) for k in range(count)]


def struct(shape, dtype):
    return jax.ShapeDtypeStruct(shape, dtype)


def split_kernel(inputs_ref, targets_ref, bias_ref, threshold_ref, out_ref, own_ref, sent_ref):
    first = lax.axis_index("core") == 0
    width, half = out_ref.shape[1:]
    block = inputs_ref[...].astype(F32)
    low, high = block[:, :half].astype(BF16), block[:, half:].astype(BF16)
    for k in range(0, out_ref.shape[0], 2):
        out_ref[k] = low
        out_ref[k + 1] = high
    block = targets_ref[...].astype(F32)
    low, high = block[:, :half], block[:, half:]
    own_ref[:width, :half] = jnp.where(first, low, high)
    sent_ref[:width, :half] = jnp.where(first, high, low)
    for ref in (own_ref, sent_ref):
        ref[width : width + 1, :width] = bias_ref[...].astype(F32)
        ref[width + 1 : width + 2, : threshold_ref.shape[1]] = threshold_ref[...]


def column(row):
    return jnp.broadcast_to(row, (8, row.shape[1])).T[:, :1]


def offset_kernel(own_ref, sent_ref, out_ref):
    first = lax.axis_index("core") == 0
    width, half = out_ref.shape
    width //= 2
    own, sent = (
        ref[:width, :half] - column(ref[width : width + 1, :])[:width] for ref in (own_ref, sent_ref)
    )
    out_ref[:width] = jnp.where(first, own, sent)
    out_ref[width:] = jnp.where(first, sent, own)


def flip_kernel(block_ref, out_ref):
    block = block_ref[...].astype(F32).T.astype(BF16)
    for k in range(out_ref.shape[0]):
        out_ref[k] = block


def encode_kernel(
    sizes, blocks_ref, own_hbm, sent_hbm, own_sides, sent_sides, whole_hbm, code_ref, own_slope, sent_slope,
    weights, whole_ref, sems,
):
    xs, zh, zl, rest, width = sizes
    latents = own_slope.shape[0]
    copies = [
        start(own_hbm, weights.at[:latents], sems.at[0]),
        start(sent_hbm, weights.at[latents:], sems.at[1]),
    ]
    for x in range(xs):
        parts = [blocks_ref[x * zl + low, :, high * rest : (high + 1) * rest] for high in range(zh) for low in range(zl)]
        size = len(parts) * rest
        whole_ref[:, x * size : (x + 1) * size] = jnp.concatenate(parts, axis=1)
    out = start(whole_ref, whole_hbm, sems.at[2])
    for copy in copies:
        copy.wait()
    bias = [column(sides[width + 1 : width + 2, :])[:latents] for sides in (own_sides, sent_sides)]
    shifted = dot(weights[...], whole_ref[...], ((1,), (1,))) - jnp.concatenate(bias, axis=0)
    sig = jax.nn.sigmoid(4.0 * shifted)
    slope = sig + 4.0 * shifted * sig * (1.0 - sig)
    own_slope[...] = slope[:latents]
    sent_slope[...] = slope[latents:]
    code = (shifted * sig).T.astype(BF16)
    for layer in range(code_ref.shape[0]):
        code_ref[layer] = code
    out.wait()


def copy_kernel(source_hbm, out_ref, sems):
    copy = start(source_hbm, out_ref, sems.at[0])
    copy.wait()


def decode_kernel(codes_ref, own_ref, sent_hbm, out_hbm, sent_ref, total_ref, out_ref, sems):
    copy = start(sent_hbm, sent_ref, sems.at[0])
    section = lax.axis_index("layer")
    layers, _, latents = codes_ref.shape
    latents //= 2
    codes = []
    for layer in range(layers):
        code = codes_ref[layer]
        codes.append(jnp.where(layer <= section, code, jnp.zeros_like(code)))
    own = jnp.concatenate([code[:, :latents] for code in codes], axis=1)
    sent = jnp.concatenate([code[:, latents:] for code in codes], axis=1)
    parts = columns(out_ref.shape[0], out_ref.shape[2])
    for k, part in enumerate(parts):
        total_ref[k] = dot(own, own_ref[:, part], ((1,), (0,)))
    copy.wait()
    results = []
    for k, part in enumerate(parts):
        out_ref[k] = (total_ref[k] + dot(sent, sent_ref[:, part], ((1,), (0,)))).astype(BF16)
        results.append(start(out_ref.at[k], out_hbm.at[k], sems.at[1 + k]))
    for copy in results:
        copy.wait()


def reduce_kernel(parts_ref, offset_ref, out_ref):
    place = lax.axis_index(FAR)
    size = offset_ref.shape[0]
    tile = jnp.concatenate([offset_ref[...].T] * (parts_ref.shape[2] // size), axis=1)
    lane = lax.broadcasted_iota(jnp.int32, tile.shape, 1)
    total = jnp.where((lane >= place * size) & (lane < (place + 1) * size), -tile, jnp.zeros_like(tile))
    for k in range(parts_ref.shape[0]):
        total += parts_ref[k].astype(F32)
    rows = out_ref.shape[1]
    for k in range(out_ref.shape[0]):
        out_ref[k] = total[k * rows : (k + 1) * rows]


def sum_kernel(parts_ref, out_ref):
    total = parts_ref[0]
    for k in range(1, parts_ref.shape[0]):
        total += parts_ref[k]
    total = total.astype(BF16)
    for k in range(out_ref.shape[0]):
        out_ref[k] = total


def error_kernel(pair, scale, positions_ref, parts_ref, out_ref):
    half = out_ref.shape[1]
    token_mask = (positions_ref[...] > 0).astype(F32)
    mask = jnp.where(lax.axis_index("core") == 0, token_mask[:, :half], token_mask[:, half:])
    totals = []
    for k in range(0, parts_ref.shape[0], pair):
        total = parts_ref[k].astype(F32)
        for j in range(k + 1, k + pair):
            total += parts_ref[j].astype(F32)
        totals.append(total)
    error = (column(mask) * jnp.concatenate(totals, axis=0) * scale).astype(BF16)
    for k in range(out_ref.shape[0]):
        out_ref[k] = error


def back_kernel(error_ref, own_ref, sent_hbm, out_ref, sent_ref, sems):
    copy = start(sent_hbm, sent_ref, sems.at[0])
    section = lax.axis_index("layer")
    first = lax.axis_index("core") == 0
    error = jnp.concatenate([error_ref[k] for k in range(error_ref.shape[0])], axis=1)
    own = dot(own_ref[...], error, ((1,), (1,)))
    copy.wait()
    sent = dot(sent_ref[...], error, ((1,), (1,)))
    latents = out_ref.shape[1]
    for layer in range(out_ref.shape[0] // 2):
        rows = slice(layer * latents, (layer + 1) * latents)
        kept = (layer <= section).astype(F32)
        out_ref[2 * layer] = (jnp.where(first, own[rows], sent[rows]) * kept).astype(BF16)
        out_ref[2 * layer + 1] = (jnp.where(first, sent[rows], own[rows]) * kept).astype(BF16)


def final_kernel(terms_ref, own_slope, sent_slope, own_ref, sent_ref, grad_hbm, threshold_ref, grad_ref, sems):
    first = lax.axis_index("core") == 0
    low, high = terms_ref[0].astype(F32), terms_ref[1].astype(F32)
    for k in range(2, terms_ref.shape[0], 2):
        low += terms_ref[k].astype(F32)
        high += terms_ref[k + 1].astype(F32)
    own = jnp.where(first, low, high) * own_slope[...]
    sent = jnp.where(first, high, low) * sent_slope[...]
    lows, highs = own.astype(BF16), sent.astype(BF16)
    results = []
    for k, part in enumerate(columns(sems.shape[0], own_ref.shape[1] // sems.shape[0])):
        grad_ref[:, part] = dot(lows, own_ref[:, part], ((1,), (0,))) + dot(highs, sent_ref[:, part], ((1,), (0,)))
        results.append(start(grad_ref.at[:, part], grad_hbm.at[:, part], sems.at[k]))
    total = -jnp.sum(own + sent, axis=1, keepdims=True)
    threshold_ref[...] = jnp.broadcast_to(total, (total.shape[0], 128)).T[:1]
    for copy in results:
        copy.wait()


def body(inputs, targets, encoder, threshold, decoders, out_bias, positions):
    layers = lax.axis_size("layer")
    width, tokens = inputs.shape[2], inputs.shape[1]
    half = tokens // 2
    latents, model = encoder.shape[1], encoder.shape[2]
    xs, zh, zl, yh = (lax.axis_size(name) for name in ("x", "zh", "zl", "yh"))
    near, far = xs * zl, zh * yh
    wide = model // near

    side = struct((width + 8, 128), F32)
    sends, own_sides, sent_sides = call(
        split_kernel,
        [struct((2 * far, width, half), BF16), side, side],
        [inputs[0].T, targets[0].T, out_bias, threshold],
        mib=62,
    )
    own_encoder = encoder[0]
    own_decoders = decoders[0].reshape(layers * latents, model)
    own_encoder = encoder[0]
    sends, own_decoders = lax.optimization_barrier((sends, decoders[0]))
    other_decoders = [swap(own_decoders[layer]) for layer in range(layers)]
    own_decoders = own_decoders.reshape(layers * latents, model)
    block = exchange(sends, FAR + ("core",)).reshape(-1, half)
    held = (block, own_encoder, own_decoders, sent_sides)
    block, sent_encoder, sent_decoders, sent_sides = lax.optimization_barrier(held)
    other_sides = swap(sent_sides)
    other_encoder = swap(sent_encoder)
    other_decoders = swap(sent_decoders)
    (sends,) = call(flip_kernel, [struct((near, half, wide), BF16)], [block])
    blocks = exchange(sends, NEAR)
    (held_decoders,) = call(
        copy_kernel,
        [struct((layers * latents, model), BF16)],
        [sent_decoders],
        scratch=[pltpu.SemaphoreType.DMA((1,))],
        remote=[0],
    )
    blocks, held_decoders = lax.optimization_barrier((blocks, held_decoders))
    whole, codes, own_slope, sent_slope = call(
        functools.partial(encode_kernel, (xs, zh, zl, wide // zh, width)),
        [
            struct((half, model), BF16),
            struct((layers, half, 2 * latents), BF16),
            struct((latents, half), F32),
            struct((latents, half), F32),
        ],
        [blocks, own_encoder, other_encoder, own_sides, other_sides],
        scratch=[
            pltpu.VMEM((2 * latents, model), BF16),
            pltpu.VMEM((half, model), BF16),
            pltpu.SemaphoreType.DMA((3,)),
        ],
        remote=[1, 2],
        remote_outs=[0],
        flops=4 * half * latents * model,
    )
    codes = exchange(codes, ("layer",))
    (offset,) = call(offset_kernel, [struct((2 * width, half), F32)], [own_sides, other_sides])
    offset = to_owner(offset)
    other_whole = swap(whole)
    other_slope = swap(sent_slope)

    (parts,) = call(
        decode_kernel,
        [struct((near, half, wide), BF16)],
        [codes, held_decoders, other_decoders],
        scratch=[
            pltpu.VMEM((layers * latents, model), BF16),
            pltpu.VMEM((near, half, wide), F32),
            pltpu.VMEM((near, half, wide), BF16),
            pltpu.SemaphoreType.DMA((1 + near,)),
        ],
        remote=[2],
        remote_outs=[0],
        mib=24,
        flops=4 * layers * half * latents * model,
    )
    parts = exchange(parts, NEAR)
    parts, offset, other_whole, other_slope = lax.optimization_barrier((parts, offset, other_whole, other_slope))
    (parts,) = call(
        reduce_kernel,
        [struct((zh, half // zh, wide), F32)],
        [parts, offset],
    )
    parts = exchange(parts, ("zh",))
    (parts,) = call(sum_kernel, [struct((far, half // zh, wide), BF16)], [parts])
    parts = exchange(parts, FAR)
    (parts,) = call(
        functools.partial(error_kernel, yh, 1.0 / layers),
        [struct((near, half, wide), BF16)],
        [positions[None], parts],
    )
    error = exchange(parts, NEAR)
    (terms,) = call(
        back_kernel,
        [struct((2 * layers, latents, half), BF16)],
        [error, held_decoders, other_decoders],
        scratch=[pltpu.VMEM((layers * latents, model), BF16), pltpu.SemaphoreType.DMA((1,))],
        remote=[2],
        flops=4 * layers * half * latents * model,
    )
    terms = exchange(terms, ("layer", "core"))
    grad_encoder, grad_threshold = call(
        final_kernel,
        [struct((latents, model), F32), struct((1, latents), F32)],
        [terms, own_slope, other_slope, whole, other_whole],
        scratch=[pltpu.VMEM((latents, model), F32), pltpu.SemaphoreType.DMA((8,))],
        remote_outs=[0],
        flops=4 * half * latents * model,
    )
    return (grad_encoder[None], grad_threshold)


LATENT = ("x", "zh", "zl", "yh", "core")


def solution(mesh, parts=(4, 4, 2, 2, 2)):
    in_specs = (
        P("layer", None, LATENT),
        P("layer", None, LATENT),
        P("layer", LATENT, None),
        P("layer", LATENT),
        P("layer", None, LATENT, None),
        P("layer", LATENT),
        P(),
    )
    out_specs = (P("layer", LATENT, None), P("layer", LATENT))
    devices = mesh.devices.reshape((mesh.devices.shape[0],) + parts)
    fine = Mesh(devices, ("layer",) + LATENT)
    return jax.shard_map(body, mesh=fine, in_specs=in_specs, out_specs=out_specs, check_vma=False)
```

```python
import functools

import jax
import jax.numpy as jnp
from jax import lax
from jax.experimental import pallas as pl
from jax.experimental.pallas import tpu as pltpu
from jax.sharding import Mesh, PartitionSpec as P

F32 = jnp.float32
BF16 = jnp.bfloat16
NEAR = ("x", "zl")
FAR = ("zh", "yh")
ANY = pl.BlockSpec(memory_space=pl.ANY)
VMEM = pl.BlockSpec(memory_space=pltpu.VMEM)
MIB = 1 << 20


def dot(left, right, dims):
    return lax.dot_general(left, right, (dims, ((), ())), preferred_element_type=F32)


def size_of(axes):
    count = 1
    for name in axes:
        count *= lax.axis_size(name)
    return count


def exchange(blocks, axes):
    return lax.all_to_all(blocks, axes, 0, 0, tiled=True)


def swap(block):
    return lax.ppermute(block, "core", [(0, 1), (1, 0)])


def to_owner(block):
    high, low = lax.axis_size("zh"), lax.axis_size("zl")
    pairs = [(a * high + b, b * low + a) for a in range(low) for b in range(high)]
    return lax.ppermute(block, ("zh", "zl"), pairs)


def call(kernel, outs, operands, later=(), scratch=(), remote=(), remote_outs=(), mib=16, flops=0):
    def run(*refs):
        kernel(*refs[: len(operands)], *refs[len(operands) + len(later) :])

    size = sum(o.size * o.dtype.itemsize for o in list(outs) + list(operands))
    return pl.pallas_call(
        run,
        out_shape=outs,
        in_specs=[ANY if k in remote else VMEM for k in range(len(operands))] + [ANY] * len(later),
        out_specs=[ANY if k in remote_outs else VMEM for k in range(len(outs))],
        scratch_shapes=scratch,
        compiler_params=pltpu.CompilerParams(vmem_limit_bytes=mib * MIB),
        cost_estimate=pl.CostEstimate(flops=flops, bytes_accessed=size, transcendentals=0),
    )(*operands, *later)


def start(source, target, semaphore):
    copy = pltpu.make_async_copy(source, target, semaphore)
    copy.start()
    return copy


def columns(count, width):
    return [slice(k * width, (k + 1) * width) for k in range(count)]


def struct(shape, dtype):
    return jax.ShapeDtypeStruct(shape, dtype)


def split_kernel(inputs_ref, targets_ref, bias_ref, threshold_ref, out_ref, own_ref, sent_ref):
    first = lax.axis_index("core") == 0
    width, half = out_ref.shape[1:]
    block = inputs_ref[...].astype(F32)
    low, high = block[:, :half].astype(BF16), block[:, half:].astype(BF16)
    for k in range(0, out_ref.shape[0], 2):
        out_ref[k] = low
        out_ref[k + 1] = high
    block = targets_ref[...].astype(F32)
    low, high = block[:, :half], block[:, half:]
    own_ref[:width, :half] = jnp.where(first, low, high)
    sent_ref[:width, :half] = jnp.where(first, high, low)
    for ref in (own_ref, sent_ref):
        ref[width : width + 1, :width] = bias_ref[...].astype(F32)
        ref[width + 1 : width + 2, : threshold_ref.shape[1]] = threshold_ref[...]


def column(row):
    return jnp.broadcast_to(row, (8, row.shape[1])).T[:, :1]


def offset_kernel(own_ref, sent_ref, out_ref):
    first = lax.axis_index("core") == 0
    width, half = out_ref.shape
    width //= 2
    own, sent = (
        ref[:width, :half] - column(ref[width : width + 1, :])[:width] for ref in (own_ref, sent_ref)
    )
    out_ref[:width] = jnp.where(first, own, sent)
    out_ref[width:] = jnp.where(first, sent, own)


def flip_kernel(block_ref, out_ref):
    block = block_ref[...].astype(F32).T.astype(BF16)
    for k in range(out_ref.shape[0]):
        out_ref[k] = block


def encode_kernel(
    sizes, blocks_ref, own_hbm, sent_hbm, own_sides, sent_sides, whole_hbm, code_ref, own_slope, sent_slope,
    weights, whole_ref, sems,
):
    xs, zh, zl, rest, width = sizes
    latents = own_slope.shape[0]
    copies = [
        start(own_hbm, weights.at[:latents], sems.at[0]),
        start(sent_hbm, weights.at[latents:], sems.at[1]),
    ]
    for x in range(xs):
        parts = [blocks_ref[x * zl + low, :, high * rest : (high + 1) * rest] for high in range(zh) for low in range(zl)]
        size = len(parts) * rest
        whole_ref[:, x * size : (x + 1) * size] = jnp.concatenate(parts, axis=1)
    out = start(whole_ref, whole_hbm, sems.at[2])
    for copy in copies:
        copy.wait()
    bias = [column(sides[width + 1 : width + 2, :])[:latents] for sides in (own_sides, sent_sides)]
    shifted = dot(weights[...], whole_ref[...], ((1,), (1,))) - jnp.concatenate(bias, axis=0)
    sig = jax.nn.sigmoid(4.0 * shifted)
    slope = sig + 4.0 * shifted * sig * (1.0 - sig)
    own_slope[...] = slope[:latents]
    sent_slope[...] = slope[latents:]
    code = (shifted * sig).T.astype(BF16)
    for layer in range(code_ref.shape[0]):
        code_ref[layer] = code
    out.wait()


def decode_kernel(codes_ref, own_hbm, sent_hbm, out_hbm, own_ref, sent_ref, total_ref, out_ref, sems):
    layers, _, latents = codes_ref.shape
    latents //= 2
    copies = []
    for k, (source, target) in enumerate(((own_hbm, own_ref), (sent_hbm, sent_ref))):
        for layer in range(layers):
            rows = slice(layer * latents, (layer + 1) * latents)
            copies.append(start(source.at[rows], target.at[rows], sems.at[k, layer]))
    section = lax.axis_index("layer")
    codes = []
    for layer in range(layers):
        code = codes_ref[layer]
        codes.append(jnp.where(layer <= section, code, jnp.zeros_like(code)))
    own = jnp.concatenate([code[:, :latents] for code in codes], axis=1)
    sent = jnp.concatenate([code[:, latents:] for code in codes], axis=1)
    parts = columns(out_ref.shape[0], out_ref.shape[2])
    for copy in copies[:layers]:
        copy.wait()
    for k, part in enumerate(parts):
        total_ref[k] = dot(own, own_ref[:, part], ((1,), (0,)))
    for copy in copies[layers:]:
        copy.wait()
    results = []
    for k, part in enumerate(parts):
        out_ref[k] = (total_ref[k] + dot(sent, sent_ref[:, part], ((1,), (0,)))).astype(BF16)
        results.append(start(out_ref.at[k], out_hbm.at[k], sems.at[2, k]))
    for copy in results:
        copy.wait()


def reduce_kernel(parts_hbm, offset_ref, out_ref, parts, sems):
    place = lax.axis_index(FAR)
    copies = [start(parts_hbm.at[k], parts.at[k], sems.at[k]) for k in range(parts.shape[0])]
    size = offset_ref.shape[0]
    tile = jnp.concatenate([offset_ref[...].T] * (parts.shape[2] // size), axis=1)
    lane = lax.broadcasted_iota(jnp.int32, tile.shape, 1)
    total = jnp.where((lane >= place * size) & (lane < (place + 1) * size), -tile, jnp.zeros_like(tile))
    for k, copy in enumerate(copies):
        copy.wait()
        total += parts[k].astype(F32)
    rows = out_ref.shape[1]
    for k in range(out_ref.shape[0]):
        out_ref[k] = total[k * rows : (k + 1) * rows]


def sum_kernel(parts_ref, out_ref):
    total = parts_ref[0]
    for k in range(1, parts_ref.shape[0]):
        total += parts_ref[k]
    total = total.astype(BF16)
    for k in range(out_ref.shape[0]):
        out_ref[k] = total


def error_kernel(pair, scale, positions_ref, parts_ref, out_ref):
    half = out_ref.shape[1]
    token_mask = (positions_ref[...] > 0).astype(F32)
    mask = jnp.where(lax.axis_index("core") == 0, token_mask[:, :half], token_mask[:, half:])
    totals = []
    for k in range(0, parts_ref.shape[0], pair):
        total = parts_ref[k].astype(F32)
        for j in range(k + 1, k + pair):
            total += parts_ref[j].astype(F32)
        totals.append(total)
    error = (column(mask) * jnp.concatenate(totals, axis=0) * scale).astype(BF16)
    for k in range(out_ref.shape[0]):
        out_ref[k] = error


def back_kernel(error_ref, own_ref, sent_ref, out_ref):
    section = lax.axis_index("layer")
    first = lax.axis_index("core") == 0
    error = jnp.concatenate([error_ref[k] for k in range(error_ref.shape[0])], axis=1)
    own = dot(own_ref[...], error, ((1,), (1,)))
    sent = dot(sent_ref[...], error, ((1,), (1,)))
    latents = out_ref.shape[1]
    for layer in range(out_ref.shape[0] // 2):
        rows = slice(layer * latents, (layer + 1) * latents)
        kept = (layer <= section).astype(F32)
        out_ref[2 * layer] = (jnp.where(first, own[rows], sent[rows]) * kept).astype(BF16)
        out_ref[2 * layer + 1] = (jnp.where(first, sent[rows], own[rows]) * kept).astype(BF16)


def final_kernel(terms_ref, own_slope, sent_slope, own_ref, sent_ref, grad_hbm, threshold_ref, grad_ref, sems):
    first = lax.axis_index("core") == 0
    low, high = terms_ref[0].astype(F32), terms_ref[1].astype(F32)
    for k in range(2, terms_ref.shape[0], 2):
        low += terms_ref[k].astype(F32)
        high += terms_ref[k + 1].astype(F32)
    own = jnp.where(first, low, high) * own_slope[...]
    sent = jnp.where(first, high, low) * sent_slope[...]
    lows, highs = own.astype(BF16), sent.astype(BF16)
    results = []
    for k, part in enumerate(columns(sems.shape[0], own_ref.shape[1] // sems.shape[0])):
        grad_ref[:, part] = dot(lows, own_ref[:, part], ((1,), (0,))) + dot(highs, sent_ref[:, part], ((1,), (0,)))
        results.append(start(grad_ref.at[:, part], grad_hbm.at[:, part], sems.at[k]))
    total = -jnp.sum(own + sent, axis=1, keepdims=True)
    threshold_ref[...] = jnp.broadcast_to(total, (total.shape[0], 128)).T[:1]
    for copy in results:
        copy.wait()


def body(inputs, targets, encoder, threshold, decoders, out_bias, positions):
    layers = lax.axis_size("layer")
    width, tokens = inputs.shape[2], inputs.shape[1]
    half = tokens // 2
    latents, model = encoder.shape[1], encoder.shape[2]
    xs, zh, zl, yh = (lax.axis_size(name) for name in ("x", "zh", "zl", "yh"))
    near, far = xs * zl, zh * yh
    wide = model // near

    side = struct((width + 8, 128), F32)
    sends, own_sides, sent_sides = call(
        split_kernel,
        [struct((2 * far, width, half), BF16), side, side],
        [inputs[0].T, targets[0].T, out_bias, threshold],
        mib=62,
    )
    own_encoder = encoder[0]
    own_decoders = decoders[0].reshape(layers * latents, model)
    own_encoder = encoder[0]
    sends, own_decoders = lax.optimization_barrier((sends, decoders[0]))
    other_decoders = [swap(own_decoders[layer]) for layer in range(layers)]
    own_decoders = own_decoders.reshape(layers * latents, model)
    block = exchange(sends, FAR + ("core",)).reshape(-1, half)
    held = (block, own_encoder, own_decoders, sent_sides)
    block, sent_encoder, sent_decoders, sent_sides = lax.optimization_barrier(held)
    other_sides = swap(sent_sides)
    other_encoder = swap(sent_encoder)
    other_decoders = swap(sent_decoders)
    (sends,) = call(flip_kernel, [struct((near, half, wide), BF16)], [block])
    blocks = exchange(sends, NEAR)
    whole, codes, own_slope, sent_slope = call(
        functools.partial(encode_kernel, (xs, zh, zl, wide // zh, width)),
        [
            struct((half, model), BF16),
            struct((layers, half, 2 * latents), BF16),
            struct((latents, half), F32),
            struct((latents, half), F32),
        ],
        [blocks, own_encoder, other_encoder, own_sides, other_sides],
        scratch=[
            pltpu.VMEM((2 * latents, model), BF16),
            pltpu.VMEM((half, model), BF16),
            pltpu.SemaphoreType.DMA((3,)),
        ],
        remote=[1, 2],
        remote_outs=[0],
        flops=4 * half * latents * model,
    )
    codes = exchange(codes, ("layer",))
    (offset,) = call(offset_kernel, [struct((2 * width, half), F32)], [own_sides, other_sides])
    offset = to_owner(offset)
    other_whole = swap(whole)
    other_slope = swap(sent_slope)

    (parts,) = call(
        decode_kernel,
        [struct((near, half, wide), BF16)],
        [codes, own_decoders, other_decoders],
        scratch=[
            pltpu.VMEM((layers * latents, model), BF16),
            pltpu.VMEM((layers * latents, model), BF16),
            pltpu.VMEM((near, half, wide), F32),
            pltpu.VMEM((near, half, wide), BF16),
            pltpu.SemaphoreType.DMA((3, near)),
        ],
        remote=[1, 2],
        remote_outs=[0],
        mib=62,
        flops=4 * layers * half * latents * model,
    )
    parts = exchange(parts, NEAR)
    parts, offset, other_whole, other_slope = lax.optimization_barrier((parts, offset, other_whole, other_slope))
    (parts,) = call(
        reduce_kernel,
        [struct((zh, half // zh, wide), F32)],
        [parts, offset],
        scratch=[pltpu.VMEM((near, half, wide), BF16), pltpu.SemaphoreType.DMA((near,))],
        remote=[0],
    )
    parts = exchange(parts, ("zh",))
    (parts,) = call(sum_kernel, [struct((far, half // zh, wide), BF16)], [parts])
    parts = exchange(parts, FAR)
    (parts,) = call(
        functools.partial(error_kernel, yh, 1.0 / layers),
        [struct((near, half, wide), BF16)],
        [positions[None], parts],
    )
    error = exchange(parts, NEAR)
    (terms,) = call(
        back_kernel,
        [struct((2 * layers, latents, half), BF16)],
        [error, own_decoders, other_decoders],
        flops=4 * layers * half * latents * model,
    )
    terms = exchange(terms, ("layer", "core"))
    grad_encoder, grad_threshold = call(
        final_kernel,
        [struct((latents, model), F32), struct((1, latents), F32)],
        [terms, own_slope, other_slope, whole, other_whole],
        scratch=[pltpu.VMEM((latents, model), F32), pltpu.SemaphoreType.DMA((8,))],
        remote_outs=[0],
        flops=4 * half * latents * model,
    )
    return (grad_encoder[None], grad_threshold)


LATENT = ("x", "zh", "zl", "yh", "core")


def solution(mesh, parts=(4, 8, 1, 2, 2)):
    in_specs = (
        P("layer", None, LATENT),
        P("layer", None, LATENT),
        P("layer", LATENT, None),
        P("layer", LATENT),
        P("layer", None, LATENT, None),
        P("layer", LATENT),
        P(),
    )
    out_specs = (P("layer", LATENT, None), P("layer", LATENT))
    devices = mesh.devices.reshape((mesh.devices.shape[0],) + parts)
    fine = Mesh(devices, ("layer",) + LATENT)
    return jax.shard_map(body, mesh=fine, in_specs=in_specs, out_specs=out_specs, check_vma=False)
```

```python
import functools

import jax
import jax.numpy as jnp
from jax import lax
from jax.experimental import pallas as pl
from jax.experimental.pallas import tpu as pltpu
from jax.sharding import Mesh, PartitionSpec as P

F32 = jnp.float32
BF16 = jnp.bfloat16
NEAR = ("x", "zl")
FAR = ("zh", "yh")
ANY = pl.BlockSpec(memory_space=pl.ANY)
VMEM = pl.BlockSpec(memory_space=pltpu.VMEM)
MIB = 1 << 20


def dot(left, right, dims):
    return lax.dot_general(left, right, (dims, ((), ())), preferred_element_type=F32)


def size_of(axes):
    count = 1
    for name in axes:
        count *= lax.axis_size(name)
    return count


def exchange(blocks, axes):
    return lax.all_to_all(blocks, axes, 0, 0, tiled=True)


def swap(block):
    return lax.ppermute(block, "core", [(0, 1), (1, 0)])


def to_owner(block):
    high, low = lax.axis_size("zh"), lax.axis_size("zl")
    pairs = [(a * high + b, b * low + a) for a in range(low) for b in range(high)]
    return lax.ppermute(block, ("zh", "zl"), pairs)


def call(kernel, outs, operands, later=(), scratch=(), remote=(), remote_outs=(), mib=16, flops=0):
    def run(*refs):
        kernel(*refs[: len(operands)], *refs[len(operands) + len(later) :])

    size = sum(o.size * o.dtype.itemsize for o in list(outs) + list(operands))
    return pl.pallas_call(
        run,
        out_shape=outs,
        in_specs=[ANY if k in remote else VMEM for k in range(len(operands))] + [ANY] * len(later),
        out_specs=[ANY if k in remote_outs else VMEM for k in range(len(outs))],
        scratch_shapes=scratch,
        compiler_params=pltpu.CompilerParams(vmem_limit_bytes=mib * MIB),
        cost_estimate=pl.CostEstimate(flops=flops, bytes_accessed=size, transcendentals=0),
    )(*operands, *later)


def start(source, target, semaphore):
    copy = pltpu.make_async_copy(source, target, semaphore)
    copy.start()
    return copy


def columns(count, width):
    return [slice(k * width, (k + 1) * width) for k in range(count)]


def struct(shape, dtype):
    return jax.ShapeDtypeStruct(shape, dtype)


def split_kernel(inputs_ref, targets_ref, bias_ref, threshold_ref, out_ref, own_ref, sent_ref):
    first = lax.axis_index("core") == 0
    width, half = out_ref.shape[1:]
    block = inputs_ref[...].astype(F32)
    low, high = block[:, :half].astype(BF16), block[:, half:].astype(BF16)
    for k in range(0, out_ref.shape[0], 2):
        out_ref[k] = low
        out_ref[k + 1] = high
    block = targets_ref[...].astype(F32)
    low, high = block[:, :half], block[:, half:]
    own_ref[:width, :half] = jnp.where(first, low, high)
    sent_ref[:width, :half] = jnp.where(first, high, low)
    for ref in (own_ref, sent_ref):
        ref[width : width + 1, :width] = bias_ref[...].astype(F32)
        ref[width + 1 : width + 2, : threshold_ref.shape[1]] = threshold_ref[...]


def column(row):
    return jnp.broadcast_to(row, (8, row.shape[1])).T[:, :1]


def offset_kernel(own_ref, sent_ref, out_ref):
    first = lax.axis_index("core") == 0
    width, half = out_ref.shape
    width //= 2
    own, sent = (
        ref[:width, :half] - column(ref[width : width + 1, :])[:width] for ref in (own_ref, sent_ref)
    )
    out_ref[:width] = jnp.where(first, own, sent)
    out_ref[width:] = jnp.where(first, sent, own)


def flip_kernel(block_ref, out_ref):
    block = block_ref[...].astype(F32).T.astype(BF16)
    for k in range(out_ref.shape[0]):
        out_ref[k] = block


def encode_kernel(
    sizes, blocks_ref, own_hbm, sent_hbm, own_sides, sent_sides, whole_hbm, code_ref, own_slope, sent_slope,
    weights, whole_ref, sems,
):
    xs, zh, zl, rest, width = sizes
    latents = own_slope.shape[0]
    copies = [
        start(own_hbm, weights.at[:latents], sems.at[0]),
        start(sent_hbm, weights.at[latents:], sems.at[1]),
    ]
    for x in range(xs):
        parts = [blocks_ref[x * zl + low, :, high * rest : (high + 1) * rest] for high in range(zh) for low in range(zl)]
        size = len(parts) * rest
        whole_ref[:, x * size : (x + 1) * size] = jnp.concatenate(parts, axis=1)
    out = start(whole_ref, whole_hbm, sems.at[2])
    for copy in copies:
        copy.wait()
    bias = [column(sides[width + 1 : width + 2, :])[:latents] for sides in (own_sides, sent_sides)]
    shifted = dot(weights[...], whole_ref[...], ((1,), (1,))) - jnp.concatenate(bias, axis=0)
    sig = jax.nn.sigmoid(4.0 * shifted)
    slope = sig + 4.0 * shifted * sig * (1.0 - sig)
    own_slope[...] = slope[:latents]
    sent_slope[...] = slope[latents:]
    code = (shifted * sig).T.astype(BF16)
    for layer in range(code_ref.shape[0]):
        code_ref[layer] = code
    out.wait()


def decode_kernel(codes_ref, own_hbm, sent_hbm, out_hbm, own_ref, sent_ref, total_ref, out_ref, sems):
    layers, _, latents = codes_ref.shape
    latents //= 2
    copies = []
    for k, (source, target) in enumerate(((own_hbm, own_ref), (sent_hbm, sent_ref))):
        for layer in range(layers):
            rows = slice(layer * latents, (layer + 1) * latents)
            copies.append(start(source.at[rows], target.at[rows], sems.at[k, layer]))
    section = lax.axis_index("layer")
    codes = []
    for layer in range(layers):
        code = codes_ref[layer]
        codes.append(jnp.where(layer <= section, code, jnp.zeros_like(code)))
    own = jnp.concatenate([code[:, :latents] for code in codes], axis=1)
    sent = jnp.concatenate([code[:, latents:] for code in codes], axis=1)
    parts = columns(out_ref.shape[0], out_ref.shape[2])
    for copy in copies[:layers]:
        copy.wait()
    for k, part in enumerate(parts):
        total_ref[k] = dot(own, own_ref[:, part], ((1,), (0,)))
    for copy in copies[layers:]:
        copy.wait()
    results = []
    for k, part in enumerate(parts):
        out_ref[k] = (total_ref[k] + dot(sent, sent_ref[:, part], ((1,), (0,)))).astype(BF16)
        results.append(start(out_ref.at[k], out_hbm.at[k], sems.at[2, k]))
    for copy in results:
        copy.wait()


def reduce_kernel(parts_ref, offset_ref, out_ref):
    place = lax.axis_index(FAR)
    size = offset_ref.shape[0]
    tile = jnp.concatenate([offset_ref[...].T] * (parts_ref.shape[2] // size), axis=1)
    lane = lax.broadcasted_iota(jnp.int32, tile.shape, 1)
    total = jnp.where((lane >= place * size) & (lane < (place + 1) * size), -tile, jnp.zeros_like(tile))
    for k in range(parts_ref.shape[0]):
        total += parts_ref[k].astype(F32)
    rows = out_ref.shape[1]
    for k in range(out_ref.shape[0]):
        out_ref[k] = total[k * rows : (k + 1) * rows]


def sum_kernel(parts_ref, out_ref):
    total = parts_ref[0]
    for k in range(1, parts_ref.shape[0]):
        total += parts_ref[k]
    total = total.astype(BF16)
    for k in range(out_ref.shape[0]):
        out_ref[k] = total


def error_kernel(pair, scale, positions_ref, parts_ref, out_ref):
    half = out_ref.shape[1]
    token_mask = (positions_ref[...] > 0).astype(F32)
    mask = jnp.where(lax.axis_index("core") == 0, token_mask[:, :half], token_mask[:, half:])
    totals = []
    for k in range(0, parts_ref.shape[0], pair):
        total = parts_ref[k].astype(F32)
        for j in range(k + 1, k + pair):
            total += parts_ref[j].astype(F32)
        totals.append(total)
    error = (column(mask) * jnp.concatenate(totals, axis=0) * scale).astype(BF16)
    for k in range(out_ref.shape[0]):
        out_ref[k] = error


def back_kernel(error_ref, own_ref, sent_ref, out_ref):
    section = lax.axis_index("layer")
    first = lax.axis_index("core") == 0
    error = jnp.concatenate([error_ref[k] for k in range(error_ref.shape[0])], axis=1)
    own = dot(own_ref[...], error, ((1,), (1,)))
    sent = dot(sent_ref[...], error, ((1,), (1,)))
    latents = out_ref.shape[1]
    for layer in range(out_ref.shape[0] // 2):
        rows = slice(layer * latents, (layer + 1) * latents)
        kept = (layer <= section).astype(F32)
        out_ref[2 * layer] = (jnp.where(first, own[rows], sent[rows]) * kept).astype(BF16)
        out_ref[2 * layer + 1] = (jnp.where(first, sent[rows], own[rows]) * kept).astype(BF16)


def final_kernel(terms_ref, own_slope, sent_slope, own_ref, sent_ref, grad_hbm, threshold_ref, grad_ref, sems):
    first = lax.axis_index("core") == 0
    low, high = terms_ref[0].astype(F32), terms_ref[1].astype(F32)
    for k in range(2, terms_ref.shape[0], 2):
        low += terms_ref[k].astype(F32)
        high += terms_ref[k + 1].astype(F32)
    own = jnp.where(first, low, high) * own_slope[...]
    sent = jnp.where(first, high, low) * sent_slope[...]
    lows, highs = own.astype(BF16), sent.astype(BF16)
    results = []
    for k, part in enumerate(columns(sems.shape[0], own_ref.shape[1] // sems.shape[0])):
        grad_ref[:, part] = dot(lows, own_ref[:, part], ((1,), (0,))) + dot(highs, sent_ref[:, part], ((1,), (0,)))
        results.append(start(grad_ref.at[:, part], grad_hbm.at[:, part], sems.at[k]))
    total = -jnp.sum(own + sent, axis=1, keepdims=True)
    threshold_ref[...] = jnp.broadcast_to(total, (total.shape[0], 128)).T[:1]
    for copy in results:
        copy.wait()


def body(inputs, targets, encoder, threshold, decoders, out_bias, positions):
    layers = lax.axis_size("layer")
    width, tokens = inputs.shape[2], inputs.shape[1]
    half = tokens // 2
    latents, model = encoder.shape[1], encoder.shape[2]
    xs, zh, zl, yh = (lax.axis_size(name) for name in ("x", "zh", "zl", "yh"))
    near, far = xs * zl, zh * yh
    wide = model // near

    side = struct((width + 8, 128), F32)
    sends, own_sides, sent_sides = call(
        split_kernel,
        [struct((2 * far, width, half), BF16), side, side],
        [inputs[0].T, targets[0].T, out_bias, threshold],
        mib=62,
    )
    own_encoder = encoder[0]
    own_decoders = decoders[0].reshape(layers * latents, model)
    own_encoder = encoder[0]
    sends, own_decoders = lax.optimization_barrier((sends, decoders[0]))
    other_decoders = [swap(own_decoders[layer]) for layer in range(layers)]
    own_decoders = own_decoders.reshape(layers * latents, model)
    sends, sent_decoders = lax.optimization_barrier((sends, own_decoders))
    other_decoders = swap(sent_decoders)
    block = exchange(sends, FAR + ("core",)).reshape(-1, half)
    held = (block, own_encoder, sent_sides)
    block, sent_encoder, sent_sides = lax.optimization_barrier(held)
    other_sides = swap(sent_sides)
    other_encoder = swap(sent_encoder)
    (sends,) = call(flip_kernel, [struct((near, half, wide), BF16)], [block])
    blocks = exchange(sends, NEAR)
    whole, codes, own_slope, sent_slope = call(
        functools.partial(encode_kernel, (xs, zh, zl, wide // zh, width)),
        [
            struct((half, model), BF16),
            struct((layers, half, 2 * latents), BF16),
            struct((latents, half), F32),
            struct((latents, half), F32),
        ],
        [blocks, own_encoder, other_encoder, own_sides, other_sides],
        scratch=[
            pltpu.VMEM((2 * latents, model), BF16),
            pltpu.VMEM((half, model), BF16),
            pltpu.SemaphoreType.DMA((3,)),
        ],
        remote=[1, 2],
        remote_outs=[0],
        flops=4 * half * latents * model,
    )
    codes = exchange(codes, ("layer",))
    (offset,) = call(offset_kernel, [struct((2 * width, half), F32)], [own_sides, other_sides])
    offset = to_owner(offset)
    other_whole = swap(whole)
    other_slope = swap(sent_slope)

    (parts,) = call(
        decode_kernel,
        [struct((near, half, wide), BF16)],
        [codes, own_decoders, other_decoders],
        scratch=[
            pltpu.VMEM((layers * latents, model), BF16),
            pltpu.VMEM((layers * latents, model), BF16),
            pltpu.VMEM((near, half, wide), F32),
            pltpu.VMEM((near, half, wide), BF16),
            pltpu.SemaphoreType.DMA((3, near)),
        ],
        remote=[1, 2],
        remote_outs=[0],
        mib=62,
        flops=4 * layers * half * latents * model,
    )
    parts = exchange(parts, NEAR)
    parts, offset, other_whole, other_slope = lax.optimization_barrier((parts, offset, other_whole, other_slope))
    (parts,) = call(
        reduce_kernel,
        [struct((zh, half // zh, wide), F32)],
        [parts, offset],
    )
    parts = exchange(parts, ("zh",))
    (parts,) = call(sum_kernel, [struct((far, half // zh, wide), BF16)], [parts])
    parts = exchange(parts, FAR)
    (parts,) = call(
        functools.partial(error_kernel, yh, 1.0 / layers),
        [struct((near, half, wide), BF16)],
        [positions[None], parts],
    )
    error = exchange(parts, NEAR)
    (terms,) = call(
        back_kernel,
        [struct((2 * layers, latents, half), BF16)],
        [error, own_decoders, other_decoders],
        flops=4 * layers * half * latents * model,
    )
    terms = exchange(terms, ("layer", "core"))
    grad_encoder, grad_threshold = call(
        final_kernel,
        [struct((latents, model), F32), struct((1, latents), F32)],
        [terms, own_slope, other_slope, whole, other_whole],
        scratch=[pltpu.VMEM((latents, model), F32), pltpu.SemaphoreType.DMA((8,))],
        remote_outs=[0],
        flops=4 * half * latents * model,
    )
    return (grad_encoder[None], grad_threshold)


LATENT = ("x", "zh", "zl", "yh", "core")


def solution(mesh, parts=(4, 4, 2, 2, 2)):
    in_specs = (
        P("layer", None, LATENT),
        P("layer", None, LATENT),
        P("layer", LATENT, None),
        P("layer", LATENT),
        P("layer", None, LATENT, None),
        P("layer", LATENT),
        P(),
    )
    out_specs = (P("layer", LATENT, None), P("layer", LATENT))
    devices = mesh.devices.reshape((mesh.devices.shape[0],) + parts)
    fine = Mesh(devices, ("layer",) + LATENT)
    return jax.shard_map(body, mesh=fine, in_specs=in_specs, out_specs=out_specs, check_vma=False)
```

```python
import functools

import jax
import jax.numpy as jnp
from jax import lax
from jax.experimental import pallas as pl
from jax.experimental.pallas import tpu as pltpu
from jax.sharding import Mesh, PartitionSpec as P

F32 = jnp.float32
BF16 = jnp.bfloat16
NEAR = ("x", "zl")
FAR = ("zh", "yh")
ANY = pl.BlockSpec(memory_space=pl.ANY)
VMEM = pl.BlockSpec(memory_space=pltpu.VMEM)
MIB = 1 << 20


def dot(left, right, dims):
    return lax.dot_general(left, right, (dims, ((), ())), preferred_element_type=F32)


def size_of(axes):
    count = 1
    for name in axes:
        count *= lax.axis_size(name)
    return count


def exchange(blocks, axes):
    return lax.all_to_all(blocks, axes, 0, 0, tiled=True)


def swap(block):
    return lax.ppermute(block, "core", [(0, 1), (1, 0)])


def to_owner(block):
    high, low = lax.axis_size("zh"), lax.axis_size("zl")
    pairs = [(a * high + b, b * low + a) for a in range(low) for b in range(high)]
    return lax.ppermute(block, ("zh", "zl"), pairs)


def call(kernel, outs, operands, later=(), scratch=(), remote=(), remote_outs=(), mib=16, flops=0):
    def run(*refs):
        kernel(*refs[: len(operands)], *refs[len(operands) + len(later) :])

    size = sum(o.size * o.dtype.itemsize for o in list(outs) + list(operands))
    return pl.pallas_call(
        run,
        out_shape=outs,
        in_specs=[ANY if k in remote else VMEM for k in range(len(operands))] + [ANY] * len(later),
        out_specs=[ANY if k in remote_outs else VMEM for k in range(len(outs))],
        scratch_shapes=scratch,
        compiler_params=pltpu.CompilerParams(vmem_limit_bytes=mib * MIB),
        cost_estimate=pl.CostEstimate(flops=flops, bytes_accessed=size, transcendentals=0),
    )(*operands, *later)


def start(source, target, semaphore):
    copy = pltpu.make_async_copy(source, target, semaphore)
    copy.start()
    return copy


def columns(count, width):
    return [slice(k * width, (k + 1) * width) for k in range(count)]


def struct(shape, dtype):
    return jax.ShapeDtypeStruct(shape, dtype)


def split_kernel(inputs_ref, targets_ref, bias_ref, threshold_ref, out_ref, own_ref, sent_ref):
    first = lax.axis_index("core") == 0
    width, half = out_ref.shape[1:]
    block = inputs_ref[...].astype(F32)
    low, high = block[:, :half].astype(BF16), block[:, half:].astype(BF16)
    for k in range(0, out_ref.shape[0], 2):
        out_ref[k] = low
        out_ref[k + 1] = high
    block = targets_ref[...].astype(F32)
    low, high = block[:, :half], block[:, half:]
    own_ref[:width, :half] = jnp.where(first, low, high)
    sent_ref[:width, :half] = jnp.where(first, high, low)
    for ref in (own_ref, sent_ref):
        ref[width : width + 1, :width] = bias_ref[...].astype(F32)
        ref[width + 1 : width + 2, : threshold_ref.shape[1]] = threshold_ref[...]


def column(row):
    return jnp.broadcast_to(row, (8, row.shape[1])).T[:, :1]


def offset_kernel(own_ref, sent_ref, out_ref):
    first = lax.axis_index("core") == 0
    width, half = out_ref.shape
    width //= 2
    own, sent = (
        ref[:width, :half] - column(ref[width : width + 1, :])[:width] for ref in (own_ref, sent_ref)
    )
    out_ref[:width] = jnp.where(first, own, sent)
    out_ref[width:] = jnp.where(first, sent, own)


def flip_kernel(block_ref, out_ref):
    block = block_ref[...].astype(F32).T.astype(BF16)
    for k in range(out_ref.shape[0]):
        out_ref[k] = block


def encode_kernel(
    sizes, blocks_ref, own_hbm, sent_hbm, own_sides, sent_sides, whole_hbm, code_ref, own_slope, sent_slope,
    weights, whole_ref, sems,
):
    xs, zh, zl, rest, width = sizes
    latents = own_slope.shape[0]
    copies = [
        start(own_hbm, weights.at[:latents], sems.at[0]),
        start(sent_hbm, weights.at[latents:], sems.at[1]),
    ]
    for x in range(xs):
        parts = [blocks_ref[x * zl + low, :, high * rest : (high + 1) * rest] for high in range(zh) for low in range(zl)]
        size = len(parts) * rest
        whole_ref[:, x * size : (x + 1) * size] = jnp.concatenate(parts, axis=1)
    out = start(whole_ref, whole_hbm, sems.at[2])
    for copy in copies:
        copy.wait()
    bias = [column(sides[width + 1 : width + 2, :])[:latents] for sides in (own_sides, sent_sides)]
    shifted = dot(weights[...], whole_ref[...], ((1,), (1,))) - jnp.concatenate(bias, axis=0)
    sig = jax.nn.sigmoid(4.0 * shifted)
    slope = sig + 4.0 * shifted * sig * (1.0 - sig)
    own_slope[...] = slope[:latents]
    sent_slope[...] = slope[latents:]
    code = (shifted * sig).T.astype(BF16)
    for layer in range(code_ref.shape[0]):
        code_ref[layer] = code
    out.wait()


def decode_kernel(codes_ref, own_hbm, sent_hbm, out_hbm, own_ref, sent_ref, total_ref, out_ref, sems):
    layers, _, latents = codes_ref.shape
    latents //= 2
    copies = []
    for k, (source, target) in enumerate(((own_hbm, own_ref), (sent_hbm, sent_ref))):
        for layer in range(layers):
            rows = slice(layer * latents, (layer + 1) * latents)
            copies.append(start(source.at[rows], target.at[rows], sems.at[k, layer]))
    section = lax.axis_index("layer")
    codes = []
    for layer in range(layers):
        code = codes_ref[layer]
        codes.append(jnp.where(layer <= section, code, jnp.zeros_like(code)))
    own = jnp.concatenate([code[:, :latents] for code in codes], axis=1)
    sent = jnp.concatenate([code[:, latents:] for code in codes], axis=1)
    parts = columns(out_ref.shape[0], out_ref.shape[2])
    for copy in copies[:layers]:
        copy.wait()
    for k, part in enumerate(parts):
        total_ref[k] = dot(own, own_ref[:, part], ((1,), (0,)))
    for copy in copies[layers:]:
        copy.wait()
    results = []
    for k, part in enumerate(parts):
        out_ref[k] = (total_ref[k] + dot(sent, sent_ref[:, part], ((1,), (0,)))).astype(BF16)
        results.append(start(out_ref.at[k], out_hbm.at[k], sems.at[2, k]))
    for copy in results:
        copy.wait()


def reduce_kernel(parts_ref, offset_ref, out_ref):
    place = lax.axis_index(FAR)
    size = offset_ref.shape[0]
    tile = jnp.concatenate([offset_ref[...].T] * (parts_ref.shape[2] // size), axis=1)
    lane = lax.broadcasted_iota(jnp.int32, tile.shape, 1)
    total = jnp.where((lane >= place * size) & (lane < (place + 1) * size), -tile, jnp.zeros_like(tile))
    for k in range(parts_ref.shape[0]):
        total += parts_ref[k].astype(F32)
    rows = out_ref.shape[1]
    for k in range(out_ref.shape[0]):
        out_ref[k] = total[k * rows : (k + 1) * rows].astype(out_ref.dtype)


def sum_kernel(parts_ref, out_ref):
    total = parts_ref[0].astype(F32)
    for k in range(1, parts_ref.shape[0]):
        total += parts_ref[k].astype(F32)
    total = total.astype(BF16)
    for k in range(out_ref.shape[0]):
        out_ref[k] = total


def error_kernel(pair, scale, positions_ref, parts_ref, out_ref):
    half = out_ref.shape[1]
    token_mask = (positions_ref[...] > 0).astype(F32)
    mask = jnp.where(lax.axis_index("core") == 0, token_mask[:, :half], token_mask[:, half:])
    totals = []
    for k in range(0, parts_ref.shape[0], pair):
        total = parts_ref[k].astype(F32)
        for j in range(k + 1, k + pair):
            total += parts_ref[j].astype(F32)
        totals.append(total)
    error = (column(mask) * jnp.concatenate(totals, axis=0) * scale).astype(BF16)
    for k in range(out_ref.shape[0]):
        out_ref[k] = error


def back_kernel(error_ref, own_ref, sent_ref, out_ref):
    section = lax.axis_index("layer")
    first = lax.axis_index("core") == 0
    error = jnp.concatenate([error_ref[k] for k in range(error_ref.shape[0])], axis=1)
    own = dot(own_ref[...], error, ((1,), (1,)))
    sent = dot(sent_ref[...], error, ((1,), (1,)))
    latents = out_ref.shape[1]
    for layer in range(out_ref.shape[0] // 2):
        rows = slice(layer * latents, (layer + 1) * latents)
        kept = (layer <= section).astype(F32)
        out_ref[2 * layer] = (jnp.where(first, own[rows], sent[rows]) * kept).astype(BF16)
        out_ref[2 * layer + 1] = (jnp.where(first, sent[rows], own[rows]) * kept).astype(BF16)


def final_kernel(terms_ref, own_slope, sent_slope, own_ref, sent_ref, grad_hbm, threshold_ref, grad_ref, sems):
    first = lax.axis_index("core") == 0
    low, high = terms_ref[0].astype(F32), terms_ref[1].astype(F32)
    for k in range(2, terms_ref.shape[0], 2):
        low += terms_ref[k].astype(F32)
        high += terms_ref[k + 1].astype(F32)
    own = jnp.where(first, low, high) * own_slope[...]
    sent = jnp.where(first, high, low) * sent_slope[...]
    lows, highs = own.astype(BF16), sent.astype(BF16)
    results = []
    for k, part in enumerate(columns(sems.shape[0], own_ref.shape[1] // sems.shape[0])):
        grad_ref[:, part] = dot(lows, own_ref[:, part], ((1,), (0,))) + dot(highs, sent_ref[:, part], ((1,), (0,)))
        results.append(start(grad_ref.at[:, part], grad_hbm.at[:, part], sems.at[k]))
    total = -jnp.sum(own + sent, axis=1, keepdims=True)
    threshold_ref[...] = jnp.broadcast_to(total, (total.shape[0], 128)).T[:1]
    for copy in results:
        copy.wait()


def body(inputs, targets, encoder, threshold, decoders, out_bias, positions):
    layers = lax.axis_size("layer")
    width, tokens = inputs.shape[2], inputs.shape[1]
    half = tokens // 2
    latents, model = encoder.shape[1], encoder.shape[2]
    xs, zh, zl, yh = (lax.axis_size(name) for name in ("x", "zh", "zl", "yh"))
    near, far = xs * zl, zh * yh
    wide = model // near

    side = struct((width + 8, 128), F32)
    sends, own_sides, sent_sides = call(
        split_kernel,
        [struct((2 * far, width, half), BF16), side, side],
        [inputs[0].T, targets[0].T, out_bias, threshold],
        mib=62,
    )
    own_encoder = encoder[0]
    own_decoders = decoders[0].reshape(layers * latents, model)
    own_encoder = encoder[0]
    sends, own_decoders = lax.optimization_barrier((sends, decoders[0]))
    other_decoders = [swap(own_decoders[layer]) for layer in range(layers)]
    own_decoders = own_decoders.reshape(layers * latents, model)
    block = exchange(sends, FAR + ("core",)).reshape(-1, half)
    held = (block, own_encoder, own_decoders, sent_sides)
    block, sent_encoder, sent_decoders, sent_sides = lax.optimization_barrier(held)
    other_sides = swap(sent_sides)
    other_encoder = swap(sent_encoder)
    other_decoders = swap(sent_decoders)
    (sends,) = call(flip_kernel, [struct((near, half, wide), BF16)], [block])
    blocks = exchange(sends, NEAR)
    whole, codes, own_slope, sent_slope = call(
        functools.partial(encode_kernel, (xs, zh, zl, wide // zh, width)),
        [
            struct((half, model), BF16),
            struct((layers, half, 2 * latents), BF16),
            struct((latents, half), F32),
            struct((latents, half), F32),
        ],
        [blocks, own_encoder, other_encoder, own_sides, other_sides],
        scratch=[
            pltpu.VMEM((2 * latents, model), BF16),
            pltpu.VMEM((half, model), BF16),
            pltpu.SemaphoreType.DMA((3,)),
        ],
        remote=[1, 2],
        remote_outs=[0],
        flops=4 * half * latents * model,
    )
    codes = exchange(codes, ("layer",))
    (offset,) = call(offset_kernel, [struct((2 * width, half), F32)], [own_sides, other_sides])
    offset = to_owner(offset)
    other_whole = swap(whole)
    other_slope = swap(sent_slope)

    (parts,) = call(
        decode_kernel,
        [struct((near, half, wide), BF16)],
        [codes, own_decoders, other_decoders],
        scratch=[
            pltpu.VMEM((layers * latents, model), BF16),
            pltpu.VMEM((layers * latents, model), BF16),
            pltpu.VMEM((near, half, wide), F32),
            pltpu.VMEM((near, half, wide), BF16),
            pltpu.SemaphoreType.DMA((3, near)),
        ],
        remote=[1, 2],
        remote_outs=[0],
        mib=62,
        flops=4 * layers * half * latents * model,
    )
    parts = exchange(parts, NEAR)
    parts, offset, other_whole, other_slope = lax.optimization_barrier((parts, offset, other_whole, other_slope))
    (parts,) = call(
        reduce_kernel,
        [struct((zh, half // zh, wide), BF16)],
        [parts, offset],
    )
    parts = exchange(parts, ("zh",))
    (parts,) = call(sum_kernel, [struct((far, half // zh, wide), BF16)], [parts])
    parts = exchange(parts, FAR)
    (parts,) = call(
        functools.partial(error_kernel, yh, 1.0 / layers),
        [struct((near, half, wide), BF16)],
        [positions[None], parts],
    )
    error = exchange(parts, NEAR)
    (terms,) = call(
        back_kernel,
        [struct((2 * layers, latents, half), BF16)],
        [error, own_decoders, other_decoders],
        flops=4 * layers * half * latents * model,
    )
    terms = exchange(terms, ("layer", "core"))
    grad_encoder, grad_threshold = call(
        final_kernel,
        [struct((latents, model), F32), struct((1, latents), F32)],
        [terms, own_slope, other_slope, whole, other_whole],
        scratch=[pltpu.VMEM((latents, model), F32), pltpu.SemaphoreType.DMA((8,))],
        remote_outs=[0],
        flops=4 * half * latents * model,
    )
    return (grad_encoder[None], grad_threshold)


LATENT = ("x", "zh", "zl", "yh", "core")


def solution(mesh, parts=(4, 4, 2, 2, 2)):
    in_specs = (
        P("layer", None, LATENT),
        P("layer", None, LATENT),
        P("layer", LATENT, None),
        P("layer", LATENT),
        P("layer", None, LATENT, None),
        P("layer", LATENT),
        P(),
    )
    out_specs = (P("layer", LATENT, None), P("layer", LATENT))
    devices = mesh.devices.reshape((mesh.devices.shape[0],) + parts)
    fine = Mesh(devices, ("layer",) + LATENT)
    return jax.shard_map(body, mesh=fine, in_specs=in_specs, out_specs=out_specs, check_vma=False)
```
